128 devices in a mesh: section: 8 (over y, core), ed: 16 (over x, z).
Axes of the slice: x: 4, y: 4, z: 4, core: 2. Of those that a mesh axis runs over, the one named last changes fastest.
Arguments:
- x_in: bfloat16 [8, 2048, 4096], P('section', 'ed')
- ids_a: int32 [8, 2048, 2], P('section', 'ed'), may hold values from 0 to 15, as said below
- gates_a: float32 [8, 2048, 2], P('section', 'ed'), may hold values from 0.1 to 1
- x_saved: bfloat16 [8, 2048, 4096], P('section', 'ed')
- ids_b: int32 [8, 2048, 2], P('section', 'ed'), may hold values from 0 to 15, as said below
- gates_b: float32 [8, 2048, 2], P('section', 'ed'), may hold values from 0.1 to 1
- dy_in: bfloat16 [8, 2048, 4096], P('section', 'ed'), may hold values from -6 to 6
- gain: float32 [8, 4096], P('section'), may hold values from 0.1 to 1.9
- w_gate: bfloat16 [8, 4096, 12288], P('section', None, 'ed'), may hold values from -0.09375 to 0.09375
- w_up: bfloat16 [8, 4096, 12288], P('section', None, 'ed'), may hold values from -0.09375 to 0.09375
- w_down: bfloat16 [8, 12288, 4096], P('section', 'ed'), may hold values from -0.0546875 to 0.0546875
Outputs:
- mixed: bfloat16 [8, 2048, 4096], P('section', 'ed')
- input_grad: bfloat16 [8, 2048, 4096], P('section', 'ed')
The draws below stay inside these ranges and needn't reach their ends.
Inputs may be any that keep to these rules, and one draw needn't show every extreme that they name: `ids_a`: each token names two different experts; among the tokens of one ed index and one section at most 32 name expert 0, at least one name it, and in every section some ed index has exactly 32. `ids_b`: each token names two different experts; among the tokens of one ed index and one section at most 32 name expert 0, at least one name it, and in every section some ed index has exactly 32.
All inputs are finite; a program needn't handle non-finite values.
Results may differ from the reference program's by a relative error of at most 0.0039.
Values may be sent and summed in bfloat16 or wider, within the bound.
A program may use at most 128 MiB of HBM per device.

```python
import math
import jax
import jax.numpy as jnp
from jax import lax

D = 4096
HID = 12288
EXPERTS = 16
TOK_DEV = 128
SECTIONS = 8
TOKENS = 2048
CAP = 32
N_ED = 16


def spread_rows(key, base, row_top, col_range):
    row_key, col_key = jax.random.split(key)
    row_scale = jnp.exp(jax.random.uniform(row_key, (SECTIONS, TOKENS, 1), jnp.float32, 0.0, math.log(row_top)))
    col_scale = jnp.exp(jax.random.uniform(col_key, (SECTIONS, 1, D), jnp.float32, -col_range, col_range))
    return (base * row_scale * col_scale / (1.6 * math.sqrt(row_top))).astype(jnp.bfloat16)


def route_draw(key):
    keys = jax.random.split(key, 6)
    counts = jax.random.randint(keys[0], (SECTIONS, N_ED), 1, CAP + 1)
    busiest = jax.random.randint(keys[1], (SECTIONS, 1), 0, N_ED)
    counts = jnp.where(jnp.arange(N_ED, dtype=jnp.int32)[None, :] == busiest, CAP, counts)
    shape = (SECTIONS, N_ED, TOK_DEV)
    scores = jax.random.randint(keys[2], shape, 0, 1 << 20) * TOK_DEV + jnp.arange(TOK_DEV, dtype=jnp.int32)
    ranking = jnp.argsort(jnp.argsort(scores, axis=-1), axis=-1)
    chosen = ranking < counts[:, :, None]
    first = jax.random.randint(keys[3], shape, 1, EXPERTS)
    offset = jax.random.randint(keys[4], shape, 1, EXPERTS - 1)
    second = (first - 1 + offset) % (EXPERTS - 1) + 1
    order = jax.random.randint(keys[5], shape, 0, 2)
    leading = jnp.where(chosen, jnp.where(order == 0, 0, first), first)
    trailing = jnp.where(chosen, jnp.where(order == 0, first, 0), second)
    return jnp.stack([leading, trailing], axis=-1).reshape(SECTIONS, TOKENS, 2).astype(jnp.int32)


def draw_ids_a(key, part):
    key = jax.random.fold_in(key, 21)
    return route_draw(key)


def draw_ids_b(key, part):
    key = jax.random.fold_in(key, 22)
    return route_draw(key)


def draw_x_in(key, part):
    key = jax.random.fold_in(key, 11)
    base_key, scale_key = jax.random.split(key)
    base = jax.random.truncated_normal(base_key, -4.0, 4.0, (SECTIONS, TOKENS, D), jnp.float32)
    return spread_rows(scale_key, base, 10.0, 0.5)


def draw_x_saved(key, part):
    key = jax.random.fold_in(key, 12)
    base_key, scale_key = jax.random.split(key)
    base = jax.random.truncated_normal(base_key, -4.0, 4.0, (SECTIONS, TOKENS, D), jnp.float32)
    return spread_rows(scale_key, base, 10.0, 0.5)


def block_levels(stream_key, extent, shards, smallest, high):
    factor_of, own = 1.0, jax.random.fold_in(stream_key, 6)
    for dim, parts in shards:
        heights = jnp.exp(jax.random.uniform(jax.random.fold_in(own, dim), (parts,), jnp.float32, smallest / len(shards), high / len(shards)))
        factor_of = factor_of * jnp.repeat(heights, extent[dim] // parts).reshape([-1 if axis == dim else 1 for axis in range(len(extent))])
    return factor_of


def scatter_about(rng, dims, deviation, bound, cuts=(), kind=jnp.bfloat16):
    entries = deviation * jax.random.normal(rng, dims, jnp.float32)
    if cuts:
        entries = entries * block_levels(rng, dims, cuts, -0.22, 0.18)
    return jnp.clip(entries, -bound, bound).astype(kind)


def setup_inputs(seed: int = 0) -> dict:
    key_of = jax.random.split(jax.random.key(seed), 12)
    return {
        "x_in": draw_x_in(jax.random.fold_in(key_of[11], 71), 0),
        "ids_a": draw_ids_a(jax.random.fold_in(key_of[11], 71), 0),
        "gates_a": jnp.clip(jnp.exp(math.log(1.0) - 2.3025851 * jax.random.uniform(key_of[2], (SECTIONS, TOKENS, 2), jnp.float32) ** block_levels(key_of[2], (SECTIONS, TOKENS, 2), ((0, 8), (1, 16)), -0.2, 0.2)), 0.1, 1.0),
        "x_saved": draw_x_saved(jax.random.fold_in(key_of[11], 71), 0),
        "ids_b": draw_ids_b(jax.random.fold_in(key_of[11], 71), 0),
        "gates_b": jnp.clip(jnp.exp(math.log(1.0) - 2.3025851 * jax.random.uniform(key_of[5], (SECTIONS, TOKENS, 2), jnp.float32) ** block_levels(key_of[5], (SECTIONS, TOKENS, 2), ((0, 8), (1, 16)), -0.2, 0.2)), 0.1, 1.0),
        "dy_in": scatter_about(key_of[6], (SECTIONS, TOKENS, D), 1.0, 6.0, ((0, 8), (1, 16))),
        "gain": jnp.clip(1.0 + 0.18 * jax.random.normal(key_of[7], (SECTIONS, D), jnp.float32), 0.1, 1.9),
        "w_gate": scatter_about(key_of[8], (SECTIONS, D, HID), D ** -0.5, 0.09375, ((0, 8), (2, 16))),
        "w_up": scatter_about(key_of[9], (SECTIONS, D, HID), D ** -0.5, 0.09375, ((0, 8), (2, 16))),
        "w_down": scatter_about(key_of[10], (SECTIONS, HID, D), HID ** -0.5, 0.0546875, ((0, 8), (1, 16))),
    }


EPSILON = 1e-06

def expert_forward(inputs, gate_weight, up_weight, down_weight):
    gate_pre = jnp.dot(inputs, gate_weight, preferred_element_type=jnp.float32)
    up_pre = jnp.dot(inputs, up_weight, preferred_element_type=jnp.float32)
    hidden = (jax.nn.silu(gate_pre) * up_pre).astype(jnp.bfloat16)
    return jnp.dot(hidden, down_weight, preferred_element_type=jnp.float32).astype(jnp.bfloat16)

def expert_backward(inputs, cotangent, gate_weight, up_weight, down_weight):
    gate_pre = jnp.dot(inputs, gate_weight, preferred_element_type=jnp.float32)
    up_pre = jnp.dot(inputs, up_weight, preferred_element_type=jnp.float32)
    sigmoid_gate = jax.nn.sigmoid(gate_pre)
    contract = (((1,), (1,)), ((), ()))
    hidden_grad = lax.dot_general(cotangent, down_weight, contract, preferred_element_type=jnp.float32)
    gate_grad = (hidden_grad * up_pre * (sigmoid_gate * (1.0 + gate_pre * (1.0 - sigmoid_gate)))).astype(jnp.bfloat16)
    up_grad = (hidden_grad * (gate_pre * sigmoid_gate)).astype(jnp.bfloat16)
    back = lax.dot_general(gate_grad, gate_weight, contract, preferred_element_type=jnp.float32)
    back = back + lax.dot_general(up_grad, up_weight, contract, preferred_element_type=jnp.float32)
    return back.astype(jnp.bfloat16)

def normalize(inputs, gain_row):
    values = inputs.astype(jnp.float32)
    scale = lax.rsqrt(lax.optimization_barrier(jnp.mean(values * values, axis=-1, keepdims=True)) + EPSILON)
    return (values, scale, (values * scale * gain_row).astype(jnp.bfloat16))

def slot_index(expert_ids):
    routed_flag = jnp.any(expert_ids == 0, axis=-1).reshape(N_ED, TOK_DEV)
    position = jnp.cumsum(routed_flag.astype(jnp.int32), axis=1).astype(jnp.int32) - 1
    source = jnp.arange(N_ED, dtype=jnp.int32)[:, None] * CAP
    slots = jnp.where(routed_flag, source + position, N_ED * CAP)
    return slots.reshape(-1).astype(jnp.int32)

def gate_share(expert_ids, gate_values):
    return lax.optimization_barrier(jnp.sum(jnp.where(expert_ids == 0, gate_values, 0.0), axis=-1))

def to_table(rows, slots):
    table = jnp.zeros((N_ED * CAP + 1, D), rows.dtype)
    table = table.at[slots].set(rows)
    return table[:N_ED * CAP]

def from_table(table, slots):
    extended = jnp.concatenate([table, jnp.zeros((1, D), table.dtype)], axis=0)
    return extended[slots]

def section_step(operands):
    input_a, route_a, weight_a, saved_input, route_b, weight_b, cotangent, gain_row, gate_weight, up_weight, down_weight = operands
    _, _, normed_a = normalize(input_a, gain_row)
    slots_a = slot_index(route_a)
    share_a = gate_share(route_a, weight_a)
    outputs = expert_forward(to_table(normed_a, slots_a), gate_weight, up_weight, down_weight)
    token_out = from_table(outputs, slots_a).astype(jnp.float32)
    mixed = (input_a.astype(jnp.float32) + share_a[:, None] * token_out).astype(jnp.bfloat16)
    values_b, scale_b, normed_b = normalize(saved_input, gain_row)
    slots_b = slot_index(route_b)
    share_b = gate_share(route_b, weight_b)
    pair_cot = (share_b[:, None] * cotangent.astype(jnp.float32)).astype(jnp.bfloat16)
    backs = expert_backward(to_table(normed_b, slots_b), to_table(pair_cot, slots_b), gate_weight, up_weight, down_weight)
    pair_back = from_table(backs, slots_b).astype(jnp.float32)
    weighted = pair_back * gain_row
    average = lax.optimization_barrier(jnp.mean(weighted * values_b, axis=-1, keepdims=True))
    input_grad = cotangent.astype(jnp.float32) + scale_b * (weighted - values_b * scale_b * scale_b * average)
    return (mixed, input_grad.astype(jnp.bfloat16))

def reference(x_in, ids_a, gates_a, x_saved, ids_b, gates_b, dy_in, gain, w_gate, w_up, w_down):
    previous = jnp.roll(x_in, 1, axis=0)
    following = jnp.roll(dy_in, -1, axis=0)
    mixed, input_grad = lax.map(section_step, (previous, ids_a, gates_a, x_saved, ids_b, gates_b, following, gain, w_gate, w_up, w_down))
    return (mixed, input_grad)
```

```python
import functools

import jax
import jax.numpy as jnp
from jax import lax
from jax.experimental import pallas as pl
from jax.experimental.pallas import tpu as pltpu
from jax.sharding import PartitionSpec as P

EPSILON = 1e-06
MESH = pl.DeviceIdType.MESH
SIDE = 4
CAP = 32
PLUS, MINUS = 0, 1
F32, BF16 = jnp.float32, jnp.bfloat16
NT = (((1,), (1,)), ((), ()))


def dot(a, b):
    return jnp.dot(a, b, preferred_element_type=F32)


def dot_nt(a, b):
    return lax.dot_general(a, b, NT, preferred_element_type=F32)


def group(table, half, first, second):
    low, high = first
    if half == 0:
        return table.at[0, low:high, second * CAP : (second + 1) * CAP]
    return table.at[1, second, low * CAP : high * CAP]


def rows_of(table, half, first, rows):
    low, high = rows
    if half == 0:
        return table.at[0, first, low:high]
    return table.at[1, 0, first * CAP + low : first * CAP + high]


def kernel(
    sections,
    route_ref, gain_ref, x_in, x_saved, dy_in, w_gate, w_up, w_down,
    mixed_out, grad_out,
    gate_w, up_w, down_w, tab_b, tab_c, tab_a,
    gate_b, up_b, gate_g, up_g, hidden,
    x_here, saved, cot,
    acc_s0, acc_s1, fin_s0, fin_s1, acc_f, fin_f,
    place_a, place_b, cols, rows_out,
    send_sem, recv_sem, local_sem,
):
    section, ed = lax.axis_index("section"), lax.axis_index("ed")
    x, z = ed // SIDE, ed % SIDE

    def at_x(step):
        return (section, (x + step + SIDE) % SIDE * SIDE + z)

    def at_z(step):
        return (section, x * SIDE + (z + step + SIDE) % SIDE)

    def at_section(step):
        return ((section + step + sections) % sections, ed)

    counter = [0]

    def remote(src, dst, device):
        k = counter[0]
        counter[0] += 1
        return pltpu.make_async_remote_copy(
            src_ref=src, dst_ref=dst, send_sem=send_sem.at[k], recv_sem=recv_sem.at[k],
            device_id=device, device_id_type=MESH,
        )

    def along(half, which, direction):
        step = 1 if direction == PLUS else -1
        on_x = (which == "f") == (half == 0)
        return at_x(step) if on_x else at_z(step)

    width = gate_w.shape[1]
    depth = gate_w.shape[0]
    part = depth // 2
    rows = SIDE * SIDE * CAP
    tokens = saved.shape[0]
    tile = min(256, width)
    half_rows = CAP // 2
    low_rows, high_rows = (0, half_rows), (half_rows, CAP)

    def gather_copies(table):
        made = {}
        for h in (0, 1):
            for d in (PLUS, MINUS):
                back = 3 if d == PLUS else 1
                rows_here = low_rows if d == PLUS else high_rows
                pair = (0, 2) if d == PLUS else (2, 4)
                f, s = along(h, "f", d), along(h, "s", d)
                made[h, d, "near"] = remote(group(table, h, (0, 1), 0), group(table, h, (back, back + 1), 0), f)
                made[h, d, "own"] = remote(group(table, h, (0, 1), 0), group(table, h, (0, 1), back), s)
                made[h, d, "far"] = remote(rows_of(table, h, back, rows_here), rows_of(table, h, 2, rows_here), f)
                made[h, d, "rest"] = remote(group(table, h, (1, 4), 0), group(table, h, (1, 4), back), s)
                made[h, d, "last"] = remote(group(table, h, pair, back), group(table, h, pair, 2), s)
        return made

    def fin_slice(t, half, direction, pair):
        low, high = pair
        if half == 0:
            return fin_s0.at[t, direction, low:high]
        return fin_s1.at[t, direction, low * CAP : high * CAP]

    def scatter_copies(table, t):
        made = {}
        for h in (0, 1):
            acc = acc_s0 if h == 0 else acc_s1
            for d in (PLUS, MINUS):
                near = 1 if d == PLUS else 3
                mine, other = ((0, 2), (2, 4)) if d == PLUS else ((2, 4), (0, 2))
                my_rows, other_rows = (low_rows, high_rows) if d == PLUS else (high_rows, low_rows)
                f, s = along(h, "f", d), along(h, "s", d)
                made[h, d, "sa"] = remote(group(table, h, mine, 2), acc.at[t, d], s)
                made[h, d, "sd"] = remote(group(table, h, other, near), fin_slice(t, h, d, other), s)
                made[h, d, "sf"] = remote(group(table, h, mine, near), fin_slice(t, h, d, mine), s)
                made[h, d, "fa"] = remote(rows_of(table, h, 2, my_rows), acc_f.at[t, h, d], f)
                made[h, d, "fd"] = remote(
                    rows_of(table, h, near, other_rows), fin_f.at[t, h, d, other_rows[0] : other_rows[1]], f
                )
                made[h, d, "ff"] = remote(
                    rows_of(table, h, near, my_rows), fin_f.at[t, h, d, my_rows[0] : my_rows[1]], f
                )
        return made

    both = [(h, d) for h in (0, 1) for d in (PLUS, MINUS)]
    copy_x = remote(x_in.at[0], x_here, at_section(1))
    copy_dy = remote(dy_in.at[0], cot, at_section(-1))
    gather_b, gather_c, gather_a = gather_copies(tab_b), gather_copies(tab_c), gather_copies(tab_a)
    scatter_b, scatter_a = scatter_copies(tab_b, 0), scatter_copies(tab_c, 1)

    def start(copies, *names):
        for name in names:
            for h, d in both:
                copies[h, d, name].start()

    def after(copies, arrived, names):
        for h, d in both:
            for name in arrived:
                copies[h, d, name].wait_recv()
            for name in names:
                copies[h, d, name].start()

    def received(copies, *names):
        for h, d in both:
            for name in names:
                copies[h, d, name].wait_recv()

    def sent(copies):
        for copy in copies.values():
            copy.wait_send()

    def far(copies):
        after(copies, ("near",), ("far",))

    def rest(copies):
        for h in (0, 1):
            for d in (PLUS, MINUS):
                copies[h, d, "far"].wait_recv()
            for d in (PLUS, MINUS):
                copies[h, d, "rest"].start()

    def last(copies):
        after(copies, ("own", "rest"), ("last",))

    def scatter_0(copies, h):
        for name in ("sa", "sd"):
            for d in (PLUS, MINUS):
                copies[h, d, name].start()

    def add_into(target, other):
        target[...] = (target[...].astype(F32) + other[...].astype(F32)).astype(BF16)

    def scatter_1(copies, table, t):
        for h, d in both:
            near = 1 if d == PLUS else 3
            mine = (0, 2) if d == PLUS else (2, 4)
            acc = acc_s0 if h == 0 else acc_s1
            copies[h, d, "sa"].wait_recv()
            add_into(group(table, h, mine, near), acc.at[t, d])
            copies[h, d, "sf"].start()

    def scatter_2(copies, table, t):
        for h in (0, 1):
            for d in (PLUS, MINUS):
                copies[h, d, "sd"].wait_recv()
                copies[h, d, "sf"].wait_recv()
            fin = fin_s0 if h == 0 else fin_s1
            total = group(table, h, (0, 4), 0)
            total[...] = (
                total[...].astype(F32) + fin[t, PLUS].astype(F32) + fin[t, MINUS].astype(F32)
            ).astype(BF16)
            for name in ("fa", "fd"):
                for d in (PLUS, MINUS):
                    copies[h, d, name].start()

    def scatter_3(copies, table, t):
        for h, d in both:
            near = 1 if d == PLUS else 3
            my_rows = low_rows if d == PLUS else high_rows
            copies[h, d, "fa"].wait_recv()
            add_into(rows_of(table, h, near, my_rows), acc_f.at[t, h, d])
            copies[h, d, "ff"].start()

    def scatter_4(copies, table, t):
        for h in (0, 1):
            for d in (PLUS, MINUS):
                copies[h, d, "fd"].wait_recv()
                copies[h, d, "ff"].wait_recv()
            total = (
                rows_of(table, h, 0, (0, CAP))[...].astype(F32)
                + fin_f[t, h, PLUS].astype(F32)
                + fin_f[t, h, MINUS].astype(F32)
            )
            rows_out[t, :, h * part : (h + 1) * part] = total.astype(BF16)

    load_saved = pltpu.make_async_copy(x_saved.at[0], saved, local_sem.at[0])
    load_saved.start()
    loads = [
        pltpu.make_async_copy(src.at[0], dst, local_sem.at[k])
        for k, (src, dst) in enumerate(((w_gate, gate_w), (w_up, up_w), (w_down, down_w)), start=1)
    ]
    barrier = pltpu.get_barrier_semaphore()
    for device in (at_x(1), at_x(-1), at_z(1), at_z(-1), at_section(1), at_section(-1)):
        pl.semaphore_signal(barrier, inc=1, device_id=device, device_id_type=MESH)

    route = route_ref[...]
    upper = (
        lax.broadcasted_iota(jnp.int32, (tokens, tokens), 0) <= lax.broadcasted_iota(jnp.int32, (tokens, tokens), 1)
    )
    diagonal = (
        lax.broadcasted_iota(jnp.int32, (tokens, tokens), 0) == lax.broadcasted_iota(jnp.int32, (tokens, tokens), 1)
    )
    count = dot(route.astype(BF16), upper.astype(BF16))
    slot_rows = lax.broadcasted_iota(jnp.int32, (CAP, tokens), 0).astype(F32)
    slot_cols = lax.broadcasted_iota(jnp.int32, (tokens, CAP), 1).astype(F32)

    def column(row):
        return jnp.sum(jnp.where(diagonal, row, 0.0), axis=1, keepdims=True)

    takes = []
    for t, place in ((0, place_a), (2, place_b)):
        code = jnp.where(route[t : t + 1] > 0.5, count[t : t + 1] - 1.0, -1.0)
        takes.append(jnp.where(code == slot_rows, 1.0, 0.0))
        place[...] = jnp.where(column(code) == slot_cols, 1.0, 0.0).astype(BF16)
    take_a, take_b = takes
    share_slot = jnp.sum(take_b * route[3:4], axis=1, keepdims=True)
    cols[...] = column(route[1:2])
    take_a, take_b = take_a.astype(BF16), take_b.astype(BF16)

    pl.semaphore_wait(barrier, 6)
    copy_x.start()
    copy_dy.start()

    def put_own(table, values):
        for h in (0, 1):
            table[h, 0, 0:CAP, :] = values[:, h * part : (h + 1) * part]

    def normed(values):
        scale = lax.rsqrt(jnp.mean(values * values, axis=-1, keepdims=True) + EPSILON)
        return (values * scale * gain_ref[...]).astype(BF16)

    load_saved.wait()
    put_own(tab_b, normed(dot(take_b, saved[...])))
    start(gather_b, "near", "own")
    for load in loads:
        load.start()
    far(gather_b)
    rest(gather_b)
    copy_dy.wait_recv()
    put_own(tab_c, (share_slot * dot(take_b, cot[...])).astype(BF16))
    start(gather_c, "near", "own")
    copy_x.wait_recv()
    put_own(tab_a, normed(dot(take_a, x_here[...])))
    last(gather_b)
    far(gather_c)
    start(gather_a, "near", "own")
    for load in loads:
        load.wait()
    received(gather_b, "last")

    def tall(table, h):
        return table[h].reshape(rows, part)

    def columns(i):
        return pl.ds(pl.multiple_of(i * tile, tile), tile)

    def project(table, weight, i):
        return dot(tall(table, 0), weight[0:part, columns(i)]) + dot(tall(table, 1), weight[part:depth, columns(i)])

    steps = width // tile

    @pl.loop(0, steps)
    def _(i):
        gate_b[:, columns(i)] = project(tab_b, gate_w, i)
        up_b[:, columns(i)] = project(tab_b, up_w, i)

        @pl.when(i == 0)
        def _():
            rest(gather_c)

    far(gather_a)
    last(gather_c)
    rest(gather_a)
    received(gather_c, "last")

    @pl.loop(0, steps)
    def _(i):
        at = columns(i)
        hidden_grad = dot_nt(tall(tab_c, 0), down_w[at, 0:part]) + dot_nt(tall(tab_c, 1), down_w[at, part:depth])
        gate = gate_b[:, at]
        sigmoid = jax.nn.sigmoid(gate)
        gate_g[:, at] = (hidden_grad * up_b[:, at] * (sigmoid * (1.0 + gate * (1.0 - sigmoid)))).astype(BF16)
        up_g[:, at] = (hidden_grad * (gate * sigmoid)).astype(BF16)

    sent(gather_b)
    for h in (0, 1):

        @pl.loop(0, part // tile)
        def _(i):
            at = pl.ds(pl.multiple_of(h * part + i * tile, tile), tile)
            back = dot_nt(gate_g[...], gate_w[at, :]) + dot_nt(up_g[...], up_w[at, :])
            tab_b[h, :, :, columns(i)] = back.astype(BF16).reshape(SIDE, SIDE * CAP, tile)

        if h == 0:
            last(gather_a)
        scatter_0(scatter_b, h)

    received(gather_a, "last")

    @pl.loop(0, steps)
    def _(i):
        gate = project(tab_a, gate_w, i)
        up = project(tab_a, up_w, i)
        hidden[:, columns(i)] = (gate * jax.nn.sigmoid(gate) * up).astype(BF16)

        @pl.when(i == 0)
        def _():
            scatter_1(scatter_b, tab_b, 0)

    sent(gather_c)
    for h in (0, 1):

        @pl.loop(0, part // tile)
        def _(i):
            at = pl.ds(pl.multiple_of(h * part + i * tile, tile), tile)
            out = dot(hidden[...], down_w[:, at])
            tab_c[h, :, :, columns(i)] = out.astype(BF16).reshape(SIDE, SIDE * CAP, tile)

        scatter_0(scatter_a, h)

    scatter_2(scatter_b, tab_b, 0)
    scatter_1(scatter_a, tab_c, 1)
    scatter_3(scatter_b, tab_b, 0)
    scatter_2(scatter_a, tab_c, 1)
    scatter_4(scatter_b, tab_b, 0)

    chunk = tokens // 4

    @pl.loop(0, 4)
    def _(i):
        at = pl.ds(pl.multiple_of(i * chunk, chunk), chunk)
        values = saved[at, :].astype(F32)
        scale = lax.rsqrt(jnp.mean(values * values, axis=-1, keepdims=True) + EPSILON)
        weighted = dot(place_b[at, :], rows_out[0]) * gain_ref[...]
        average = jnp.mean(weighted * values, axis=-1, keepdims=True)
        grad = cot[at, :].astype(F32) + scale * (weighted - values * scale * scale * average)
        cot[at, :] = grad.astype(BF16)

    write_grad = pltpu.make_async_copy(cot, grad_out.at[0], local_sem.at[4])
    write_grad.start()
    scatter_3(scatter_a, tab_c, 1)
    scatter_4(scatter_a, tab_c, 1)

    @pl.loop(0, 4)
    def _(i):
        at = pl.ds(pl.multiple_of(i * chunk, chunk), chunk)
        out = dot(place_a[at, :], rows_out[1])
        x_here[at, :] = (x_here[at, :].astype(F32) + cols[at, :] * out).astype(BF16)

    write_mixed = pltpu.make_async_copy(x_here, mixed_out.at[0], local_sem.at[5])
    write_mixed.start()
    sent(gather_a)
    sent(scatter_b)
    sent(scatter_a)
    copy_x.wait_send()
    copy_dy.wait_send()
    write_grad.wait()
    write_mixed.wait()


def routing(expert_ids, gate_values):
    chosen = expert_ids == 0
    flag = jnp.any(chosen, axis=1).astype(F32)
    return flag, jnp.sum(jnp.where(chosen, gate_values, 0.0), axis=1)


def shards(sections, x_in, ids_a, gates_a, x_saved, ids_b, gates_b, dy_in, gain, w_gate, w_up, w_down):
    route = jnp.stack(routing(ids_a[0], gates_a[0]) + routing(ids_b[0], gates_b[0]))
    route = jnp.concatenate([route, jnp.zeros_like(route)], axis=0)
    _, tokens, depth = x_in.shape
    width = w_gate.shape[2]
    rows, part = SIDE * SIDE * CAP, depth // 2
    copies = 2 + 3 * 20 + 2 * 24
    table = pltpu.VMEM((2, SIDE, SIDE * CAP, part), BF16)
    flops = 8 * 2 * rows * depth * width
    anywhere, vmem = pl.BlockSpec(memory_space=pl.ANY), pl.BlockSpec(memory_space=pltpu.VMEM)
    return pl.pallas_call(
        functools.partial(kernel, sections),
        out_shape=[jax.ShapeDtypeStruct(x_in.shape, BF16)] * 2,
        in_specs=[vmem, vmem] + [anywhere] * 6,
        out_specs=[anywhere] * 2,
        scratch_shapes=[
            pltpu.VMEM((depth, width), BF16),
            pltpu.VMEM((depth, width), BF16),
            pltpu.VMEM((width, depth), BF16),
            table, table, table,
            pltpu.VMEM((rows, width), F32),
            pltpu.VMEM((rows, width), F32),
            pltpu.VMEM((rows, width), BF16),
            pltpu.VMEM((rows, width), BF16),
            pltpu.VMEM((rows, width), BF16),
            pltpu.VMEM((tokens, depth), BF16),
            pltpu.VMEM((tokens, depth), BF16),
            pltpu.VMEM((tokens, depth), BF16),
            pltpu.VMEM((2, 2, 2, CAP, part), BF16),
            pltpu.VMEM((2, 2, 2 * CAP, part), BF16),
            pltpu.VMEM((2, 2, SIDE, CAP, part), BF16),
            pltpu.VMEM((2, 2, SIDE * CAP, part), BF16),
            pltpu.VMEM((2, 2, 2, CAP // 2, part), BF16),
            pltpu.VMEM((2, 2, 2, CAP, part), BF16),
            pltpu.VMEM((tokens, CAP), BF16),
            pltpu.VMEM((tokens, CAP), BF16),
            pltpu.VMEM((tokens, 1), F32),
            pltpu.VMEM((2, CAP, depth), BF16),
            pltpu.SemaphoreType.DMA((copies,)),
            pltpu.SemaphoreType.DMA((copies,)),
            pltpu.SemaphoreType.DMA((6,)),
        ],
        compiler_params=pltpu.CompilerParams(
            collective_id=0, has_side_effects=True, vmem_limit_bytes=60 * 1024 * 1024
        ),
        cost_estimate=pl.CostEstimate(
            flops=flops, bytes_accessed=3 * depth * width * 2 + 5 * tokens * depth * 2, transcendentals=2 * rows * width
        ),
    )(route, gain, x_in, x_saved, dy_in, w_gate, w_up, w_down)


def solution(mesh):
    tokens = P("section", "ed", None)
    return jax.shard_map(
        functools.partial(shards, mesh.shape["section"]),
        mesh=mesh,
        in_specs=(tokens,) * 7
        + (P("section", None), P("section", None, "ed"), P("section", None, "ed"), P("section", "ed", None)),
        out_specs=(tokens, tokens),
        check_vma=False,
    )
```

```python
import functools

import jax
import jax.numpy as jnp
from jax import lax
from jax.experimental import pallas as pl
from jax.experimental.pallas import tpu as pltpu
from jax.sharding import PartitionSpec as P

EPSILON = 1e-06
MESH = pl.DeviceIdType.MESH
SIDE = 4
CAP = 32
PLUS, MINUS = 0, 1
PLAN = {
    "early": ('b1', 'b2', 'dy', 'c0', 'b3', 'c1', 'b4', 'x', 'c2', 'b5', 'c3', 'a0'),
    "project b": {0: ('c4',), 1: ('a1',)},
    "before hidden": ('c5',),
    "hidden grad": {0: ('a2',), 2: ('a3',)},
    "back 0": {4: ('a4',)},
    "back 1": {},
    "before project a": ("a5",),
    "project a": {1: ("sb1",)},
    "down 0": {},
    "down 1": {},
}
F32, BF16 = jnp.float32, jnp.bfloat16
NT = (((1,), (1,)), ((), ()))


def dot(a, b):
    return jnp.dot(a, b, preferred_element_type=F32)


def dot_nt(a, b):
    return lax.dot_general(a, b, NT, preferred_element_type=F32)


def group(table, half, first, second):
    low, high = first
    if half == 0:
        return table.at[0, low:high, second * CAP : (second + 1) * CAP]
    return table.at[1, second, low * CAP : high * CAP]


def rows_of(table, half, first, rows):
    low, high = rows
    if half == 0:
        return table.at[0, first, low:high]
    return table.at[1, 0, first * CAP + low : first * CAP + high]


def flag_and_share(ids, gates):
    chosen = ids[...] == 0
    return (
        jnp.sum(jnp.where(chosen, 1.0, 0.0), axis=0, keepdims=True),
        jnp.sum(jnp.where(chosen, gates[...], 0.0), axis=0, keepdims=True),
    )


def column(row):
    n = row.shape[1]
    rows, columns = lax.broadcasted_iota(jnp.int32, (n, n), 0), lax.broadcasted_iota(jnp.int32, (n, n), 1)
    return jnp.sum(jnp.where(rows == columns, row, 0.0), axis=1, keepdims=True)


def slot_code(flag):
    n = flag.shape[1]
    rows, columns = lax.broadcasted_iota(jnp.int32, (n, n), 0), lax.broadcasted_iota(jnp.int32, (n, n), 1)
    count = jnp.sum(jnp.where(rows <= columns, column(flag), 0.0), axis=0, keepdims=True)
    return jnp.where(flag > 0.5, count - 1.0, -1.0)


def kernel(
    sections,
    ids_a, gates_a, ids_b, gates_b, gain_ref, x_in, x_saved, dy_in, w_gate, w_up, w_down,
    x_out, grad_out, rows_a_out,
    gate_w, up_w, down_w, tab_b, tab_c, tab_a,
    gate_b, up_b, gate_g, up_g, hidden,
    x_here, saved, cot,
    acc_s0, acc_s1, fin_s0, fin_s1, acc_f, fin_f,
    place_b, rows_out,
    send_sem, recv_sem, local_sem,
):
    section, ed = lax.axis_index("section"), lax.axis_index("ed")
    x, z = ed // SIDE, ed % SIDE

    def at_x(step):
        return (section, (x + step + SIDE) % SIDE * SIDE + z)

    def at_z(step):
        return (section, x * SIDE + (z + step + SIDE) % SIDE)

    def at_section(step):
        return ((section + step + sections) % sections, ed)

    counter = [0]

    def remote(src, dst, device):
        k = counter[0]
        counter[0] += 1
        return pltpu.make_async_remote_copy(
            src_ref=src, dst_ref=dst, send_sem=send_sem.at[k], recv_sem=recv_sem.at[k],
            device_id=device, device_id_type=MESH,
        )

    def along(half, which, direction):
        step = 1 if direction == PLUS else -1
        on_x = (which == "f") == (half == 0)
        return at_x(step) if on_x else at_z(step)

    width = gate_w.shape[1]
    depth = gate_w.shape[0]
    part = depth // 2
    rows = SIDE * SIDE * CAP
    tokens = saved.shape[0]
    tile = min(256, width)
    half_rows = CAP // 2
    low_rows, high_rows = (0, half_rows), (half_rows, CAP)

    def gather_copies(table):
        made = {}
        for h in (0, 1):
            for d in (PLUS, MINUS):
                back = 2 if d == PLUS else 1
                rows_here = low_rows if d == PLUS else high_rows
                first = 0 if d == PLUS else 2
                f, s = along(h, "f", d), along(h, "s", d)
                made[h, d, "near"] = remote(group(table, h, (0, 1), 0), group(table, h, (back, back + 1), 0), f)
                made[h, d, "own"] = remote(group(table, h, (0, 1), 0), group(table, h, (0, 1), back), s)
                made[h, d, "far"] = remote(rows_of(table, h, back, rows_here), rows_of(table, h, 3, rows_here), f)
                made[h, d, "beside"] = remote(group(table, h, (1, 3), 0), group(table, h, (1, 3), back), s)
                made[h, d, "across"] = remote(group(table, h, (3, 4), 0), group(table, h, (3, 4), back), s)
                for name, p in (("pass_0", first), ("pass_1", first + 1)):
                    made[h, d, name] = remote(group(table, h, (p, p + 1), back), group(table, h, (p, p + 1), 3), s)
        return made

    def fin_slice(t, half, direction, pair):
        low, high = pair
        if half == 0:
            return fin_s0.at[t, direction, low:high]
        return fin_s1.at[t, direction, low * CAP : high * CAP]

    def acc_slice(t, half, direction, low):
        if half == 0:
            return acc_s0.at[t, direction, low : low + 1]
        return acc_s1.at[t, direction, low * CAP : (low + 1) * CAP]

    def scatter_copies(table, t):
        made = {}
        for h in (0, 1):
            acc = acc_s0 if h == 0 else acc_s1
            for d in (PLUS, MINUS):
                near = 1 if d == PLUS else 2
                mine, other = ((0, 2), (2, 4)) if d == PLUS else ((2, 4), (0, 2))
                my_rows, other_rows = (low_rows, high_rows) if d == PLUS else (high_rows, low_rows)
                f, s = along(h, "f", d), along(h, "s", d)
                made[h, d, "sa"] = remote(group(table, h, mine, 3), acc.at[t, d], s)
                made[h, d, "sd"] = remote(group(table, h, other, near), fin_slice(t, h, d, other), s)
                for name, p in (("sf_0", mine[0] + 1), ("sf_1", mine[0])):
                    made[h, d, name] = remote(group(table, h, (p, p + 1), near), fin_slice(t, h, d, (p, p + 1)), s)
                made[h, d, "fa"] = remote(rows_of(table, h, 3, my_rows), acc_f.at[t, h, d], f)
                made[h, d, "fd"] = remote(
                    rows_of(table, h, near, other_rows), fin_f.at[t, h, d, other_rows[0] : other_rows[1]], f
                )
                made[h, d, "ff"] = remote(
                    rows_of(table, h, near, my_rows), fin_f.at[t, h, d, my_rows[0] : my_rows[1]], f
                )
        return made

    both = [(h, d) for h in (0, 1) for d in (PLUS, MINUS)]
    copy_x = remote(x_in.at[0], x_here, at_section(1))
    copy_dy = remote(dy_in.at[0], cot, at_section(-1))
    gather_b, gather_c, gather_a = gather_copies(tab_b), gather_copies(tab_c), gather_copies(tab_a)
    scatter_b, scatter_a = scatter_copies(tab_b, 0), scatter_copies(tab_c, 1)

    def sent(copies):
        for copy in copies.values():
            copy.wait_send()

    def gather_0(copies):
        for name in ("near", "own"):
            for h, d in both:
                copies[h, d, name].start()

    def gather_1(copies):
        for h in (0, 1):
            for d in (PLUS, MINUS):
                copies[h, d, "near"].wait_recv()
                copies[h, d, "far"].start()
            for d in (PLUS, MINUS):
                copies[h, d, "beside"].start()

    def gather_2(copies):
        for h in (0, 1):
            for d in (PLUS, MINUS):
                copies[h, d, "far"].wait_recv()
            for d in (PLUS, MINUS):
                copies[h, d, "across"].start()
                copies[h, d, "own"].wait_recv()
            copies[h, PLUS, "pass_0"].start()

    def gather_3(copies):
        for h, d in both:
            copies[h, d, "beside"].wait_recv()
            copies[h, d, "pass_1" if d == PLUS else "pass_0"].start()

    def gather_4(copies):
        for h, d in both:
            copies[h, d, "across"].wait_recv()
            if d == MINUS:
                copies[h, d, "pass_1"].start()

    def gather_5(copies):
        for h, d in both:
            copies[h, d, "pass_0"].wait_recv()
            copies[h, d, "pass_1"].wait_recv()

    def scatter_0(copies, h):
        for name in ("sa", "sd"):
            for d in (PLUS, MINUS):
                copies[h, d, name].start()

    def add_into(target, other):
        target[...] = (target[...].astype(F32) + other[...].astype(F32)).astype(BF16)

    def scatter_1(copies, table, t):
        for h in (0, 1):
            for d in (PLUS, MINUS):
                copies[h, d, "sa"].wait_recv()
            for name, offset in (("sf_0", 1), ("sf_1", 0)):
                for d in (PLUS, MINUS):
                    near, p = (1, offset) if d == PLUS else (2, 2 + offset)
                    add_into(group(table, h, (p, p + 1), near), acc_slice(t, h, d, offset))
                    copies[h, d, name].start()

    def total(table, t, h, p):
        target = group(table, h, (p, p + 1), 0)
        one, two = fin_slice(t, h, PLUS, (p, p + 1)), fin_slice(t, h, MINUS, (p, p + 1))
        target[...] = (target[...].astype(F32) + one[...].astype(F32) + two[...].astype(F32)).astype(BF16)

    def scatter_2(copies, table, t):
        for h in (0, 1):
            for d in (PLUS, MINUS):
                copies[h, d, "sd"].wait_recv()
                copies[h, d, "sf_0"].wait_recv()
            total(table, t, h, 3)
            for d in (PLUS, MINUS):
                copies[h, d, "fa"].start()
            total(table, t, h, 1)
            copies[h, PLUS, "fd"].start()
        for h in (0, 1):
            copies[h, MINUS, "sf_1"].wait_recv()
            total(table, t, h, 2)
            copies[h, MINUS, "fd"].start()

    def scatter_3(copies, table, t):
        for h, d in both:
            near = 1 if d == PLUS else 2
            my_rows = low_rows if d == PLUS else high_rows
            copies[h, d, "fa"].wait_recv()
            add_into(rows_of(table, h, near, my_rows), acc_f.at[t, h, d])
            copies[h, d, "ff"].start()

    def scatter_own(copies, table, t):
        for h in (0, 1):
            copies[h, PLUS, "sf_1"].wait_recv()
            total(table, t, h, 0)

    def scatter_4(copies, table, t):
        for h in (0, 1):
            for d in (PLUS, MINUS):
                copies[h, d, "fd"].wait_recv()
                copies[h, d, "ff"].wait_recv()
            out = (
                rows_of(table, h, 0, (0, CAP))[...].astype(F32)
                + fin_f[t, h, PLUS].astype(F32)
                + fin_f[t, h, MINUS].astype(F32)
            )
            rows_out[t, :, h * part : (h + 1) * part] = out.astype(BF16)

    load_saved = pltpu.make_async_copy(x_saved.at[0], saved, local_sem.at[0])
    load_saved.start()
    loads = [
        pltpu.make_async_copy(src.at[0], dst, local_sem.at[k])
        for k, (src, dst) in enumerate(((w_gate, gate_w), (w_up, up_w), (w_down, down_w)), start=1)
    ]
    keep_x = pltpu.make_async_copy(x_here, x_out, local_sem.at[6])
    barrier = pltpu.get_barrier_semaphore()
    for device in (at_x(1), at_x(-1), at_z(1), at_z(-1), at_section(1), at_section(-1)):
        pl.semaphore_signal(barrier, inc=1, device_id=device, device_id_type=MESH)

    flag_a, share_a = flag_and_share(ids_a, gates_a)
    flag_b, share_b = flag_and_share(ids_b, gates_b)
    slot_rows = lax.broadcasted_iota(jnp.int32, (CAP, tokens), 0).astype(F32)
    slot_cols = lax.broadcasted_iota(jnp.int32, (tokens, CAP), 1).astype(F32)
    code_b = slot_code(flag_b)
    take_a = jnp.where(slot_code(flag_a) == slot_rows, 1.0, 0.0).astype(BF16)
    take_b = jnp.where(code_b == slot_rows, 1.0, 0.0)
    share_slot = jnp.sum(take_b * share_b, axis=1, keepdims=True)
    take_b = take_b.astype(BF16)
    place_b[...] = jnp.where(column(code_b) == slot_cols, 1.0, 0.0).astype(BF16)

    pl.semaphore_wait(barrier, 6)
    copy_x.start()
    copy_dy.start()

    def put_own(table, values):
        for h in (0, 1):
            table[h, 0, 0:CAP, :] = values[:, h * part : (h + 1) * part]

    def normed(values):
        scale = lax.rsqrt(jnp.mean(values * values, axis=-1, keepdims=True) + EPSILON)
        return (values * scale * gain_ref[...]).astype(BF16)

    load_saved.wait()
    put_own(tab_b, normed(dot(take_b, saved[...])))
    def rows_c():
        copy_dy.wait_recv()
        put_own(tab_c, (share_slot * dot(take_b, cot[...])).astype(BF16))

    def rows_a():
        copy_x.wait_recv()
        keep_x.start()
        put_own(tab_a, normed(dot(take_a, x_here[...])))

    gather = (gather_0, gather_1, gather_2, gather_3, gather_4, gather_5)
    steps = {"dy": rows_c, "x": rows_a}
    for name, copies in (("a", gather_a), ("b", gather_b), ("c", gather_c)):
        for k, step in enumerate(gather):
            steps[f"{name}{k}"] = functools.partial(step, copies)
    scatter = {1: scatter_1, 2: scatter_2, 3: scatter_3, 4: scatter_4, 5: scatter_own}
    for name, copies, table, t in (("a", scatter_a, tab_c, 1), ("b", scatter_b, tab_b, 0)):
        for k, step in scatter.items():
            steps[f"s{name}{k}"] = functools.partial(step, copies, table, t)

    def do(*names):
        for name in names:
            steps[name]()

    def during(label, i):
        for k, names in PLAN[label].items():

            @pl.when(i == k)
            def _():
                do(*names)

    do("b0")
    for load in loads:
        load.start()
    do(*PLAN["early"])
    for load in loads:
        load.wait()

    def tall(table, h):
        return table[h].reshape(rows, part)

    def columns(i):
        return pl.ds(pl.multiple_of(i * tile, tile), tile)

    def project(table, weight, i):
        return dot(tall(table, 0), weight[0:part, columns(i)]) + dot(tall(table, 1), weight[part:depth, columns(i)])

    count = width // tile

    @pl.loop(0, count)
    def _(i):
        gate_b[:, columns(i)] = project(tab_b, gate_w, i)
        up_b[:, columns(i)] = project(tab_b, up_w, i)
        during("project b", i)

    do(*PLAN["before hidden"])

    @pl.loop(0, count)
    def _(i):
        at = columns(i)
        hidden_grad = dot_nt(tall(tab_c, 0), down_w[at, 0:part]) + dot_nt(tall(tab_c, 1), down_w[at, part:depth])
        gate = gate_b[:, at]
        sigmoid = jax.nn.sigmoid(gate)
        gate_g[:, at] = (hidden_grad * up_b[:, at] * (sigmoid * (1.0 + gate * (1.0 - sigmoid)))).astype(BF16)
        up_g[:, at] = (hidden_grad * (gate * sigmoid)).astype(BF16)
        during("hidden grad", i)

    sent(gather_b)
    for h in (0, 1):

        @pl.loop(0, part // tile)
        def _(i):
            at = pl.ds(pl.multiple_of(h * part + i * tile, tile), tile)
            back = dot_nt(gate_g[...], gate_w[at, :]) + dot_nt(up_g[...], up_w[at, :])
            tab_b[h, :, :, columns(i)] = back.astype(BF16).reshape(SIDE, SIDE * CAP, tile)
            during(f"back {h}", i)

        scatter_0(scatter_b, h)

    do(*PLAN["before project a"])

    @pl.loop(0, count)
    def _(i):
        gate = project(tab_a, gate_w, i)
        up = project(tab_a, up_w, i)
        hidden[:, columns(i)] = (gate * jax.nn.sigmoid(gate) * up).astype(BF16)
        during("project a", i)

    sent(gather_c)
    for h in (0, 1):

        @pl.loop(0, part // tile)
        def _(i):
            at = pl.ds(pl.multiple_of(h * part + i * tile, tile), tile)
            out = dot(hidden[...], down_w[:, at])
            tab_c[h, :, :, columns(i)] = out.astype(BF16).reshape(SIDE, SIDE * CAP, tile)
            during(f"down {h}", i)

        scatter_0(scatter_a, h)

    scatter_2(scatter_b, tab_b, 0)
    scatter_1(scatter_a, tab_c, 1)
    scatter_3(scatter_b, tab_b, 0)
    scatter_own(scatter_b, tab_b, 0)
    scatter_2(scatter_a, tab_c, 1)
    scatter_4(scatter_b, tab_b, 0)

    chunk = tokens // 4

    def grad_part(i):
        at = pl.ds(pl.multiple_of(i * chunk, chunk), chunk)
        values = saved[at, :].astype(F32)
        scale = lax.rsqrt(jnp.mean(values * values, axis=-1, keepdims=True) + EPSILON)
        weighted = dot(place_b[at, :], rows_out[0]) * gain_ref[...]
        average = jnp.mean(weighted * values, axis=-1, keepdims=True)
        grad = cot[at, :].astype(F32) + scale * (weighted - values * scale * scale * average)
        cot[at, :] = grad.astype(BF16)

    pl.loop(0, 2)(grad_part)
    scatter_3(scatter_a, tab_c, 1)
    pl.loop(2, 4)(grad_part)
    write_grad = pltpu.make_async_copy(cot, grad_out, local_sem.at[4])
    write_grad.start()
    scatter_own(scatter_a, tab_c, 1)
    scatter_4(scatter_a, tab_c, 1)
    write_rows = pltpu.make_async_copy(rows_out.at[1], rows_a_out, local_sem.at[5])
    write_rows.start()
    sent(gather_a)
    sent(scatter_b)
    sent(scatter_a)
    copy_x.wait_send()
    copy_dy.wait_send()
    keep_x.wait()
    write_grad.wait()
    write_rows.wait()


def finish(ids_a, gates_a, x_here, rows_a, grad, mixed_out, grad_out, x_part, grad_part, rows, sem):
    tokens = x_part.shape[0]
    chunk = tokens // 4
    load_rows = pltpu.make_async_copy(rows_a, rows, sem.at[8])
    load_rows.start()
    chunks = [pl.ds(i * chunk, chunk) for i in range(4)]
    wide = x_part.shape[1] // 4
    strips = [pl.ds(i * wide, wide) for i in range(4)]
    loads = [pltpu.make_async_copy(x_here.at[:, at], x_part.at[:, at], sem.at[i]) for i, at in enumerate(strips)]
    takes = [pltpu.make_async_copy(grad.at[at], grad_part.at[at], sem.at[4 + i]) for i, at in enumerate(chunks)]
    for copy in loads + takes:
        copy.start()
    flag, share = flag_and_share(ids_a, gates_a)
    place = (column(slot_code(flag)) == lax.broadcasted_iota(jnp.int32, (tokens, CAP), 1).astype(F32)).astype(F32)
    place = place.astype(BF16)
    share = column(share)
    load_rows.wait()
    writes = []
    for i, (at, strip) in enumerate(zip(chunks, strips)):
        loads[i].wait()
        x_part[:, strip] = (x_part[:, strip].astype(F32) + share * dot(place, rows[:, strip])).astype(BF16)
        writes.append(pltpu.make_async_copy(x_part.at[:, strip], mixed_out.at[0, :, strip], sem.at[9 + i]))
        writes[-1].start()
        takes[i].wait()
        writes.append(pltpu.make_async_copy(grad_part.at[at], grad_out.at[0, at], sem.at[13 + i]))
        writes[-1].start()
    for write in writes:
        write.wait()


def shards(sections, x_in, ids_a, gates_a, x_saved, ids_b, gates_b, dy_in, gain, w_gate, w_up, w_down):
    _, tokens, depth = x_in.shape
    width = w_gate.shape[2]
    rows, part = SIDE * SIDE * CAP, depth // 2
    copies = 2 + 3 * 28 + 2 * 28
    table = pltpu.VMEM((2, SIDE, SIDE * CAP, part), BF16)
    flops = 8 * 2 * rows * depth * width
    anywhere, vmem = pl.BlockSpec(memory_space=pl.ANY), pl.BlockSpec(memory_space=pltpu.VMEM)
    block = jax.ShapeDtypeStruct((tokens, depth), BF16)
    routes = ids_a[0].T, gates_a[0].T, ids_b[0].T, gates_b[0].T
    x_here, grad, rows_a = pl.pallas_call(
        functools.partial(kernel, sections),
        out_shape=[block, block, jax.ShapeDtypeStruct((CAP, depth), BF16)],
        in_specs=[vmem] * 5 + [anywhere] * 6,
        out_specs=[anywhere] * 3,
        scratch_shapes=[
            pltpu.VMEM((depth, width), BF16),
            pltpu.VMEM((depth, width), BF16),
            pltpu.VMEM((width, depth), BF16),
            table, table, table,
            pltpu.VMEM((rows, width), F32),
            pltpu.VMEM((rows, width), F32),
            pltpu.VMEM((rows, width), BF16),
            pltpu.VMEM((rows, width), BF16),
            pltpu.VMEM((rows, width), BF16),
            pltpu.VMEM((tokens, depth), BF16),
            pltpu.VMEM((tokens, depth), BF16),
            pltpu.VMEM((tokens, depth), BF16),
            pltpu.VMEM((2, 2, 2, CAP, part), BF16),
            pltpu.VMEM((2, 2, 2 * CAP, part), BF16),
            pltpu.VMEM((2, 2, SIDE, CAP, part), BF16),
            pltpu.VMEM((2, 2, SIDE * CAP, part), BF16),
            pltpu.VMEM((2, 2, 2, CAP // 2, part), BF16),
            pltpu.VMEM((2, 2, 2, CAP, part), BF16),
            pltpu.VMEM((tokens, CAP), BF16),
            pltpu.VMEM((2, CAP, depth), BF16),
            pltpu.SemaphoreType.DMA((copies,)),
            pltpu.SemaphoreType.DMA((copies,)),
            pltpu.SemaphoreType.DMA((7,)),
        ],
        compiler_params=pltpu.CompilerParams(
            collective_id=0, has_side_effects=True, vmem_limit_bytes=60 * 1024 * 1024
        ),
        cost_estimate=pl.CostEstimate(
            flops=flops, bytes_accessed=3 * depth * width * 2 + 5 * tokens * depth * 2, transcendentals=2 * rows * width
        ),
    )(*routes, gain, x_in, x_saved, dy_in, w_gate, w_up, w_down)
    return pl.pallas_call(
        finish,
        out_shape=[jax.ShapeDtypeStruct(x_in.shape, BF16)] * 2,
        in_specs=[vmem] * 2 + [anywhere] * 3,
        out_specs=[anywhere] * 2,
        scratch_shapes=[
            pltpu.VMEM((tokens, depth), BF16),
            pltpu.VMEM((tokens, depth), BF16),
            pltpu.VMEM((CAP, depth), BF16),
            pltpu.SemaphoreType.DMA((17,)),
        ],
        compiler_params=pltpu.CompilerParams(vmem_limit_bytes=60 * 1024 * 1024),
    )(routes[0], routes[1], x_here, rows_a, grad)


def solution(mesh):
    tokens = P("section", "ed", None)
    return jax.shard_map(
        functools.partial(shards, mesh.shape["section"]),
        mesh=mesh,
        in_specs=(tokens,) * 7
        + (P("section", None), P("section", None, "ed"), P("section", None, "ed"), P("section", "ed", None)),
        out_specs=(tokens, tokens),
        check_vma=False,
    )
```

```python
import functools

import jax
import jax.numpy as jnp
from jax import lax
from jax.experimental import pallas as pl
from jax.experimental.pallas import tpu as pltpu
from jax.sharding import PartitionSpec as P

EPSILON = 1e-06
MESH = pl.DeviceIdType.MESH
SIDE = 4
CAP = 32
PLUS, MINUS = 0, 1
PLAN = {
    "early": ("b1", "b2", "dy", "c0", "b3", "c1", "b4", "c2", "x", "b5", "c3", "a0", "c4"),
    "project b": {0: ("a1",)},
    "before hidden": ("c5",),
    "hidden grad": {0: ("a2",), 1: ("a3",)},
    "back 0": {0: ("a4",)},
    "back 1": {},
    "before project a": ("a5",),
    "project a": {1: ("sb1",)},
    "down 0": {},
    "down 1": {},
}
F32, BF16 = jnp.float32, jnp.bfloat16
NT = (((1,), (1,)), ((), ()))


def dot(a, b):
    return jnp.dot(a, b, preferred_element_type=F32)


def dot_nt(a, b):
    return lax.dot_general(a, b, NT, preferred_element_type=F32)


def group(table, half, first, second):
    low, high = first
    if half == 0:
        return table.at[0, low:high, second * CAP : (second + 1) * CAP]
    return table.at[1, second, low * CAP : high * CAP]


def rows_of(table, half, first, rows):
    low, high = rows
    if half == 0:
        return table.at[0, first, low:high]
    return table.at[1, 0, first * CAP + low : first * CAP + high]


def flag_and_share(ids, gates):
    chosen = ids[...] == 0
    return (
        jnp.sum(jnp.where(chosen, 1.0, 0.0), axis=0, keepdims=True),
        jnp.sum(jnp.where(chosen, gates[...], 0.0), axis=0, keepdims=True),
    )


def column(row):
    n = row.shape[1]
    rows, columns = lax.broadcasted_iota(jnp.int32, (n, n), 0), lax.broadcasted_iota(jnp.int32, (n, n), 1)
    return jnp.sum(jnp.where(rows == columns, row, 0.0), axis=1, keepdims=True)


def slot_code(flag):
    n = flag.shape[1]
    rows, columns = lax.broadcasted_iota(jnp.int32, (n, n), 0), lax.broadcasted_iota(jnp.int32, (n, n), 1)
    count = jnp.sum(jnp.where(rows <= columns, column(flag), 0.0), axis=0, keepdims=True)
    return jnp.where(flag > 0.5, count - 1.0, -1.0)


def kernel(
    sections,
    ids_a_in, gates_a_in, ids_b_in, gates_b_in, gain_in, x_in, x_saved, dy_in, w_gate, w_up, w_down,
    x_out, grad_out, rows_a_out,
    gate_w, up_w, down_w, tab_b, tab_c, tab_a,
    gate_b, up_b, gate_g, up_g, hidden,
    x_here, saved, cot,
    acc_s0, acc_s1, fin_s0, fin_s1, acc_f, fin_f,
    place_b, rows_out, ids_a, gates_a, ids_b, gates_b, gain_ref,
    send_sem, recv_sem, local_sem, small_sem,
):
    section, ed = lax.axis_index("section"), lax.axis_index("ed")
    x, z = ed // SIDE, ed % SIDE

    def at_x(step):
        return (section, (x + step + SIDE) % SIDE * SIDE + z)

    def at_z(step):
        return (section, x * SIDE + (z + step + SIDE) % SIDE)

    def at_section(step):
        return ((section + step + sections) % sections, ed)

    counter = [0]

    def remote(src, dst, device):
        k = counter[0]
        counter[0] += 1
        return pltpu.make_async_remote_copy(
            src_ref=src, dst_ref=dst, send_sem=send_sem.at[k], recv_sem=recv_sem.at[k],
            device_id=device, device_id_type=MESH,
        )

    def along(half, which, direction):
        step = 1 if direction == PLUS else -1
        on_x = (which == "f") == (half == 0)
        return at_x(step) if on_x else at_z(step)

    width = gate_w.shape[1]
    depth = gate_w.shape[0]
    part = depth // 2
    rows = SIDE * SIDE * CAP
    tokens = saved.shape[0]
    tile = min(256, width)
    half_rows = CAP // 2
    low_rows, high_rows = (0, half_rows), (half_rows, CAP)

    def gather_copies(table):
        made = {}
        for h in (0, 1):
            for d in (PLUS, MINUS):
                back = 2 if d == PLUS else 1
                rows_here = low_rows if d == PLUS else high_rows
                first = 0 if d == PLUS else 2
                f, s = along(h, "f", d), along(h, "s", d)
                made[h, d, "near"] = remote(group(table, h, (0, 1), 0), group(table, h, (back, back + 1), 0), f)
                made[h, d, "own"] = remote(group(table, h, (0, 1), 0), group(table, h, (0, 1), back), s)
                made[h, d, "far"] = remote(rows_of(table, h, back, rows_here), rows_of(table, h, 3, rows_here), f)
                made[h, d, "beside"] = remote(group(table, h, (1, 3), 0), group(table, h, (1, 3), back), s)
                made[h, d, "across"] = remote(group(table, h, (3, 4), 0), group(table, h, (3, 4), back), s)
                for name, p in (("pass_0", first), ("pass_1", first + 1)):
                    made[h, d, name] = remote(group(table, h, (p, p + 1), back), group(table, h, (p, p + 1), 3), s)
        return made

    def fin_slice(t, half, direction, pair):
        low, high = pair
        if half == 0:
            return fin_s0.at[t, direction, low:high]
        return fin_s1.at[t, direction, low * CAP : high * CAP]

    def acc_slice(t, half, direction, low):
        if half == 0:
            return acc_s0.at[t, direction, low : low + 1]
        return acc_s1.at[t, direction, low * CAP : (low + 1) * CAP]

    def scatter_copies(table, t):
        made = {}
        for h in (0, 1):
            acc = acc_s0 if h == 0 else acc_s1
            for d in (PLUS, MINUS):
                near = 1 if d == PLUS else 2
                mine, other = ((0, 2), (2, 4)) if d == PLUS else ((2, 4), (0, 2))
                my_rows, other_rows = (low_rows, high_rows) if d == PLUS else (high_rows, low_rows)
                f, s = along(h, "f", d), along(h, "s", d)
                made[h, d, "sa"] = remote(group(table, h, mine, 3), acc.at[t, d], s)
                made[h, d, "sd"] = remote(group(table, h, other, near), fin_slice(t, h, d, other), s)
                for name, p in (("sf_0", mine[0] + 1), ("sf_1", mine[0])):
                    made[h, d, name] = remote(group(table, h, (p, p + 1), near), fin_slice(t, h, d, (p, p + 1)), s)
                made[h, d, "fa"] = remote(rows_of(table, h, 3, my_rows), acc_f.at[t, h, d], f)
                made[h, d, "fd"] = remote(
                    rows_of(table, h, near, other_rows), fin_f.at[t, h, d, other_rows[0] : other_rows[1]], f
                )
                made[h, d, "ff"] = remote(
                    rows_of(table, h, near, my_rows), fin_f.at[t, h, d, my_rows[0] : my_rows[1]], f
                )
        return made

    both = [(h, d) for h in (0, 1) for d in (PLUS, MINUS)]
    copy_x = remote(x_in.at[0], x_here, at_section(1))
    copy_dy = remote(dy_in.at[0], cot, at_section(-1))
    gather_b, gather_c, gather_a = gather_copies(tab_b), gather_copies(tab_c), gather_copies(tab_a)
    scatter_b, scatter_a = scatter_copies(tab_b, 0), scatter_copies(tab_c, 1)

    def sent(copies):
        for copy in copies.values():
            copy.wait_send()

    def gather_0(copies):
        for name in ("near", "own"):
            for h, d in both:
                copies[h, d, name].start()

    def gather_1(copies):
        for h in (0, 1):
            for d in (PLUS, MINUS):
                copies[h, d, "near"].wait_recv()
                copies[h, d, "far"].start()
            for d in (PLUS, MINUS):
                copies[h, d, "beside"].start()

    def gather_2(copies):
        for h in (0, 1):
            for d in (PLUS, MINUS):
                copies[h, d, "far"].wait_recv()
            for d in (PLUS, MINUS):
                copies[h, d, "across"].start()
                copies[h, d, "own"].wait_recv()
            copies[h, PLUS, "pass_0"].start()

    def gather_3(copies):
        for h, d in both:
            copies[h, d, "beside"].wait_recv()
            copies[h, d, "pass_1" if d == PLUS else "pass_0"].start()

    def gather_4(copies):
        for h, d in both:
            copies[h, d, "across"].wait_recv()
            if d == MINUS:
                copies[h, d, "pass_1"].start()

    def gather_5(copies):
        for h, d in both:
            copies[h, d, "pass_0"].wait_recv()
            copies[h, d, "pass_1"].wait_recv()

    def scatter_0(copies, h):
        for name in ("sa", "sd"):
            for d in (PLUS, MINUS):
                copies[h, d, name].start()

    def add_into(target, other):
        target[...] = (target[...].astype(F32) + other[...].astype(F32)).astype(BF16)

    def scatter_1(copies, table, t):
        for h in (0, 1):
            for d in (PLUS, MINUS):
                copies[h, d, "sa"].wait_recv()
            for name, offset in (("sf_0", 1), ("sf_1", 0)):
                for d in (PLUS, MINUS):
                    near, p = (1, offset) if d == PLUS else (2, 2 + offset)
                    add_into(group(table, h, (p, p + 1), near), acc_slice(t, h, d, offset))
                    copies[h, d, name].start()

    def total(table, t, h, p):
        target = group(table, h, (p, p + 1), 0)
        one, two = fin_slice(t, h, PLUS, (p, p + 1)), fin_slice(t, h, MINUS, (p, p + 1))
        target[...] = (target[...].astype(F32) + one[...].astype(F32) + two[...].astype(F32)).astype(BF16)

    def scatter_2(copies, table, t):
        for h in (0, 1):
            for d in (PLUS, MINUS):
                copies[h, d, "sd"].wait_recv()
                copies[h, d, "sf_0"].wait_recv()
            total(table, t, h, 3)
            for d in (PLUS, MINUS):
                copies[h, d, "fa"].start()
            total(table, t, h, 1)
            copies[h, PLUS, "fd"].start()
        for h in (0, 1):
            copies[h, MINUS, "sf_1"].wait_recv()
            total(table, t, h, 2)
            copies[h, MINUS, "fd"].start()

    def scatter_3(copies, table, t):
        for h, d in both:
            near = 1 if d == PLUS else 2
            my_rows = low_rows if d == PLUS else high_rows
            copies[h, d, "fa"].wait_recv()
            add_into(rows_of(table, h, near, my_rows), acc_f.at[t, h, d])
            copies[h, d, "ff"].start()

    def scatter_own(copies, table, t):
        for h in (0, 1):
            copies[h, PLUS, "sf_1"].wait_recv()
            total(table, t, h, 0)

    def scatter_4(copies, table, t):
        for h in (0, 1):
            for d in (PLUS, MINUS):
                copies[h, d, "fd"].wait_recv()
                copies[h, d, "ff"].wait_recv()
            out = (
                rows_of(table, h, 0, (0, CAP))[...].astype(F32)
                + fin_f[t, h, PLUS].astype(F32)
                + fin_f[t, h, MINUS].astype(F32)
            )
            rows_out[t, :, h * part : (h + 1) * part] = out.astype(BF16)

    barrier = pltpu.get_barrier_semaphore()
    for device in (at_x(1), at_x(-1), at_z(1), at_z(-1), at_section(1), at_section(-1)):
        pl.semaphore_signal(barrier, inc=1, device_id=device, device_id_type=MESH)
    small = [
        pltpu.make_async_copy(src, dst, small_sem.at[k])
        for k, (src, dst) in enumerate(
            ((ids_b_in, ids_b), (gates_b_in, gates_b), (ids_a_in, ids_a), (gates_a_in, gates_a), (gain_in, gain_ref))
        )
    ]
    load_saved = pltpu.make_async_copy(x_saved.at[0], saved, local_sem.at[0])
    load_saved.start()
    for copy in small:
        copy.start()
    loads = [
        pltpu.make_async_copy(src.at[0], dst, local_sem.at[k])
        for k, (src, dst) in enumerate(((w_gate, gate_w), (w_up, up_w), (w_down, down_w)), start=1)
    ]
    keep_x = pltpu.make_async_copy(x_here, x_out, local_sem.at[6])

    for copy in small:
        copy.wait()
    flag_a, share_a = flag_and_share(ids_a, gates_a)
    flag_b, share_b = flag_and_share(ids_b, gates_b)
    slot_rows = lax.broadcasted_iota(jnp.int32, (CAP, tokens), 0).astype(F32)
    slot_cols = lax.broadcasted_iota(jnp.int32, (tokens, CAP), 1).astype(F32)
    code_b = slot_code(flag_b)
    take_a = jnp.where(slot_code(flag_a) == slot_rows, 1.0, 0.0).astype(BF16)
    take_b = jnp.where(code_b == slot_rows, 1.0, 0.0)
    share_slot = jnp.sum(take_b * share_b, axis=1, keepdims=True)
    take_b = take_b.astype(BF16)
    place_b[...] = jnp.where(column(code_b) == slot_cols, 1.0, 0.0).astype(BF16)


    def put_own(table, values):
        for h in (0, 1):
            table[h, 0, 0:CAP, :] = values[:, h * part : (h + 1) * part]

    def normed(values):
        scale = lax.rsqrt(jnp.mean(values * values, axis=-1, keepdims=True) + EPSILON)
        return (values * scale * gain_ref[...]).astype(BF16)

    load_saved.wait()
    put_own(tab_b, normed(dot(take_b, saved[...])))
    def rows_c():
        copy_dy.wait_recv()
        put_own(tab_c, (share_slot * dot(take_b, cot[...])).astype(BF16))

    def rows_a():
        copy_x.wait_recv()
        keep_x.start()
        put_own(tab_a, normed(dot(take_a, x_here[...])))

    gather = (gather_0, gather_1, gather_2, gather_3, gather_4, gather_5)
    steps = {"dy": rows_c, "x": rows_a}
    for name, copies in (("a", gather_a), ("b", gather_b), ("c", gather_c)):
        for k, step in enumerate(gather):
            steps[f"{name}{k}"] = functools.partial(step, copies)
    scatter = {1: scatter_1, 2: scatter_2, 3: scatter_3, 4: scatter_4, 5: scatter_own}
    for name, copies, table, t in (("a", scatter_a, tab_c, 1), ("b", scatter_b, tab_b, 0)):
        for k, step in scatter.items():
            steps[f"s{name}{k}"] = functools.partial(step, copies, table, t)

    def do(*names):
        for name in names:
            steps[name]()

    def during(label, i):
        for k, names in PLAN[label].items():

            @pl.when(i == k)
            def _():
                do(*names)

    pl.semaphore_wait(barrier, 6)
    copy_x.start()
    copy_dy.start()
    do("b0")
    for load in loads:
        load.start()
    do(*PLAN["early"])
    for load in loads:
        load.wait()

    def tall(table, h):
        return table[h].reshape(rows, part)

    def strip(i, size):
        return pl.ds(pl.multiple_of(i * size, size), size)

    def columns(i):
        return strip(i, tile)

    def project(table, weight, i):
        return dot(tall(table, 0), weight[0:part, columns(i)]) + dot(tall(table, 1), weight[part:depth, columns(i)])

    count = width // tile

    @pl.loop(0, count)
    def _(i):
        gate_b[:, columns(i)] = project(tab_b, gate_w, i)
        up_b[:, columns(i)] = project(tab_b, up_w, i)
        during("project b", i)

    do(*PLAN["before hidden"])

    @pl.loop(0, 2)
    def _(i):
        at = strip(i, width // 2)
        hidden_grad = dot_nt(tall(tab_c, 0), down_w[at, 0:part]) + dot_nt(tall(tab_c, 1), down_w[at, part:depth])
        gate = gate_b[:, at]
        sigmoid = jax.nn.sigmoid(gate)
        gate_g[:, at] = (hidden_grad * up_b[:, at] * (sigmoid * (1.0 + gate * (1.0 - sigmoid)))).astype(BF16)
        up_g[:, at] = (hidden_grad * (gate * sigmoid)).astype(BF16)
        during("hidden grad", i)

    sent(gather_b)
    for h in (0, 1):

        @pl.loop(0, 2)
        def _(i):
            at = strip(2 * h + i, part // 2)
            back = dot_nt(gate_g[...], gate_w[at, :]) + dot_nt(up_g[...], up_w[at, :])
            tab_b[h, :, :, strip(i, part // 2)] = back.astype(BF16).reshape(SIDE, SIDE * CAP, part // 2)
            during(f"back {h}", i)

        scatter_0(scatter_b, h)

    do(*PLAN["before project a"])

    @pl.loop(0, count)
    def _(i):
        gate = project(tab_a, gate_w, i)
        up = project(tab_a, up_w, i)
        hidden[:, columns(i)] = (gate * jax.nn.sigmoid(gate) * up).astype(BF16)
        during("project a", i)

    sent(gather_c)
    for h in (0, 1):

        @pl.loop(0, 2)
        def _(i):
            at = strip(2 * h + i, part // 2)
            out = dot(hidden[...], down_w[:, at])
            tab_c[h, :, :, strip(i, part // 2)] = out.astype(BF16).reshape(SIDE, SIDE * CAP, part // 2)
            during(f"down {h}", i)

        scatter_0(scatter_a, h)

    scatter_2(scatter_b, tab_b, 0)
    scatter_1(scatter_a, tab_c, 1)
    scatter_3(scatter_b, tab_b, 0)
    scatter_own(scatter_b, tab_b, 0)
    scatter_2(scatter_a, tab_c, 1)
    scatter_4(scatter_b, tab_b, 0)

    chunk = tokens // 4

    def grad_part(i):
        at = pl.ds(pl.multiple_of(i * chunk, chunk), chunk)
        values = saved[at, :].astype(F32)
        scale = lax.rsqrt(jnp.mean(values * values, axis=-1, keepdims=True) + EPSILON)
        weighted = dot(place_b[at, :], rows_out[0]) * gain_ref[...]
        average = jnp.mean(weighted * values, axis=-1, keepdims=True)
        grad = cot[at, :].astype(F32) + scale * (weighted - values * scale * scale * average)
        cot[at, :] = grad.astype(BF16)

    pl.loop(0, 2)(grad_part)
    scatter_3(scatter_a, tab_c, 1)
    pl.loop(2, 4)(grad_part)
    write_grad = pltpu.make_async_copy(cot, grad_out, local_sem.at[4])
    write_grad.start()
    scatter_own(scatter_a, tab_c, 1)
    scatter_4(scatter_a, tab_c, 1)
    write_rows = pltpu.make_async_copy(rows_out.at[1], rows_a_out, local_sem.at[5])
    write_rows.start()
    sent(gather_a)
    sent(scatter_b)
    sent(scatter_a)
    copy_x.wait_send()
    copy_dy.wait_send()
    keep_x.wait()
    write_grad.wait()
    write_rows.wait()


def finish(ids_in, gates_in, x_here, rows_a, grad, mixed_out, grad_out, ids_a, gates_a, x_part, grad_part, rows, sem):
    tokens = x_part.shape[0]
    chunk = tokens // 4
    load_rows = pltpu.make_async_copy(rows_a, rows, sem.at[8])
    load_ids = pltpu.make_async_copy(ids_in, ids_a, sem.at[17])
    load_gates = pltpu.make_async_copy(gates_in, gates_a, sem.at[18])
    for copy in (load_ids, load_gates, load_rows):
        copy.start()
    chunks = [pl.ds(i * chunk, chunk) for i in range(4)]
    wide = x_part.shape[1] // 4
    strips = [pl.ds(i * wide, wide) for i in range(4)]
    loads = [pltpu.make_async_copy(x_here.at[:, at], x_part.at[:, at], sem.at[i]) for i, at in enumerate(strips)]
    takes = [pltpu.make_async_copy(grad.at[at], grad_part.at[at], sem.at[4 + i]) for i, at in enumerate(chunks)]
    for copy in loads + takes:
        copy.start()
    load_ids.wait()
    load_gates.wait()
    flag, share = flag_and_share(ids_a, gates_a)
    place = (column(slot_code(flag)) == lax.broadcasted_iota(jnp.int32, (tokens, CAP), 1).astype(F32)).astype(F32)
    place = place.astype(BF16)
    share = column(share)
    load_rows.wait()
    writes = []
    for i, (at, strip) in enumerate(zip(chunks, strips)):
        loads[i].wait()
        x_part[:, strip] = (x_part[:, strip].astype(F32) + share * dot(place, rows[:, strip])).astype(BF16)
        writes.append(pltpu.make_async_copy(x_part.at[:, strip], mixed_out.at[0, :, strip], sem.at[9 + i]))
        writes[-1].start()
        takes[i].wait()
        writes.append(pltpu.make_async_copy(grad_part.at[at], grad_out.at[0, at], sem.at[13 + i]))
        writes[-1].start()
    for write in writes:
        write.wait()


def shards(sections, x_in, ids_a, gates_a, x_saved, ids_b, gates_b, dy_in, gain, w_gate, w_up, w_down):
    _, tokens, depth = x_in.shape
    width = w_gate.shape[2]
    rows, part = SIDE * SIDE * CAP, depth // 2
    copies = 2 + 3 * 28 + 2 * 28
    table = pltpu.VMEM((2, SIDE, SIDE * CAP, part), BF16)
    flops = 8 * 2 * rows * depth * width
    anywhere = pl.BlockSpec(memory_space=pl.ANY)
    block = jax.ShapeDtypeStruct((tokens, depth), BF16)
    routes = ids_a[0].T, gates_a[0].T, ids_b[0].T, gates_b[0].T
    x_here, grad, rows_a = pl.pallas_call(
        functools.partial(kernel, sections),
        out_shape=[block, block, jax.ShapeDtypeStruct((CAP, depth), BF16)],
        in_specs=[anywhere] * 11,
        out_specs=[anywhere] * 3,
        scratch_shapes=[
            pltpu.VMEM((depth, width), BF16),
            pltpu.VMEM((depth, width), BF16),
            pltpu.VMEM((width, depth), BF16),
            table, table, table,
            pltpu.VMEM((rows, width), F32),
            pltpu.VMEM((rows, width), F32),
            pltpu.VMEM((rows, width), BF16),
            pltpu.VMEM((rows, width), BF16),
            pltpu.VMEM((rows, width), BF16),
            pltpu.VMEM((tokens, depth), BF16),
            pltpu.VMEM((tokens, depth), BF16),
            pltpu.VMEM((tokens, depth), BF16),
            pltpu.VMEM((2, 2, 2, CAP, part), BF16),
            pltpu.VMEM((2, 2, 2 * CAP, part), BF16),
            pltpu.VMEM((2, 2, SIDE, CAP, part), BF16),
            pltpu.VMEM((2, 2, SIDE * CAP, part), BF16),
            pltpu.VMEM((2, 2, 2, CAP // 2, part), BF16),
            pltpu.VMEM((2, 2, 2, CAP, part), BF16),
            pltpu.VMEM((tokens, CAP), BF16),
            pltpu.VMEM((2, CAP, depth), BF16),
            pltpu.VMEM((2, tokens), jnp.int32),
            pltpu.VMEM((2, tokens), F32),
            pltpu.VMEM((2, tokens), jnp.int32),
            pltpu.VMEM((2, tokens), F32),
            pltpu.VMEM((1, depth), F32),
            pltpu.SemaphoreType.DMA((copies,)),
            pltpu.SemaphoreType.DMA((copies,)),
            pltpu.SemaphoreType.DMA((7,)),
            pltpu.SemaphoreType.DMA((5,)),
        ],
        compiler_params=pltpu.CompilerParams(
            collective_id=0, has_side_effects=True, vmem_limit_bytes=60 * 1024 * 1024
        ),
        cost_estimate=pl.CostEstimate(
            flops=flops, bytes_accessed=3 * depth * width * 2 + 5 * tokens * depth * 2, transcendentals=2 * rows * width
        ),
    )(*routes, gain, x_in, x_saved, dy_in, w_gate, w_up, w_down)
    return pl.pallas_call(
        finish,
        out_shape=[jax.ShapeDtypeStruct(x_in.shape, BF16)] * 2,
        in_specs=[anywhere] * 5,
        out_specs=[anywhere] * 2,
        scratch_shapes=[
            pltpu.VMEM((2, tokens), jnp.int32),
            pltpu.VMEM((2, tokens), F32),
            pltpu.VMEM((tokens, depth), BF16),
            pltpu.VMEM((tokens, depth), BF16),
            pltpu.VMEM((CAP, depth), BF16),
            pltpu.SemaphoreType.DMA((19,)),
        ],
        compiler_params=pltpu.CompilerParams(vmem_limit_bytes=60 * 1024 * 1024),
    )(routes[0], routes[1], x_here, rows_a, grad)


def solution(mesh):
    tokens = P("section", "ed", None)
    return jax.shard_map(
        functools.partial(shards, mesh.shape["section"]),
        mesh=mesh,
        in_specs=(tokens,) * 7
        + (P("section", None), P("section", None, "ed"), P("section", None, "ed"), P("section", "ed", None)),
        out_specs=(tokens, tokens),
        check_vma=False,
    )
```

```python
import functools

import jax
import jax.numpy as jnp
from jax import lax
from jax.experimental import pallas as pl
from jax.experimental.pallas import tpu as pltpu
from jax.sharding import PartitionSpec as P

EPSILON = 1e-06
MESH = pl.DeviceIdType.MESH
SIDE = 4
CAP = 32
PLUS, MINUS = 0, 1
PLAN = {
    "early": ("b1", "b2", "dy", "c0", "b3", "c1", "b4", "c2", "x", "b5", "c3", "a0", "c4"),
    "project b": {0: ("a1",)},
    "before hidden": ("c5",),
    "hidden grad": {0: ("a2",), 1: ("a3",)},
    "back 0": {0: ("a4",)},
    "back 1": {},
    "before project a": ("a5",),
    "project a": {1: ("sb1",)},
    "down 0": {},
    "down 1": {},
}
F32, BF16 = jnp.float32, jnp.bfloat16
NT = (((1,), (1,)), ((), ()))


def dot(a, b):
    return jnp.dot(a, b, preferred_element_type=F32)


def dot_nt(a, b):
    return lax.dot_general(a, b, NT, preferred_element_type=F32)


def group(table, half, first, second):
    low, high = first
    if half == 0:
        return table.at[0, low:high, second * CAP : (second + 1) * CAP]
    return table.at[1, second, low * CAP : high * CAP]


def rows_of(table, half, first, rows):
    low, high = rows
    if half == 0:
        return table.at[0, first, low:high]
    return table.at[1, 0, first * CAP + low : first * CAP + high]


def flag_and_share(ids, gates):
    chosen = ids[...] == 0
    return (
        jnp.sum(jnp.where(chosen, 1.0, 0.0), axis=0, keepdims=True),
        jnp.sum(jnp.where(chosen, gates[...], 0.0), axis=0, keepdims=True),
    )


def column(row):
    n = row.shape[1]
    rows, columns = lax.broadcasted_iota(jnp.int32, (n, n), 0), lax.broadcasted_iota(jnp.int32, (n, n), 1)
    return jnp.sum(jnp.where(rows == columns, row, 0.0), axis=1, keepdims=True)


def slot_code(flag):
    n = flag.shape[1]
    rows, columns = lax.broadcasted_iota(jnp.int32, (n, n), 0), lax.broadcasted_iota(jnp.int32, (n, n), 1)
    count = jnp.sum(jnp.where(rows <= columns, column(flag), 0.0), axis=0, keepdims=True)
    return jnp.where(flag > 0.5, count - 1.0, -1.0)


def kernel(
    sections,
    ids_a_in, gates_a_in, ids_b_in, gates_b_in, gain_in, x_in, x_saved, dy_in, w_gate, w_up, w_down,
    x_out, grad_out, rows_a_out,
    gate_w, up_w, down_w, tab_b, tab_c, tab_a,
    gate_b, up_b, gate_g, up_g, hidden,
    x_here, saved, cot,
    acc_s0, acc_s1, fin_s0, fin_s1, acc_f, fin_f,
    place_b, rows_out, ids_a, gates_a, ids_b, gates_b, gain_ref,
    send_sem, recv_sem, local_sem, small_sem,
):
    section, ed = lax.axis_index("section"), lax.axis_index("ed")
    x, z = ed // SIDE, ed % SIDE

    def at_x(step):
        return (section, (x + step + SIDE) % SIDE * SIDE + z)

    def at_z(step):
        return (section, x * SIDE + (z + step + SIDE) % SIDE)

    def at_section(step):
        return ((section + step + sections) % sections, ed)

    counter = [0]

    def remote(src, dst, device):
        k = counter[0]
        counter[0] += 1
        return pltpu.make_async_remote_copy(
            src_ref=src, dst_ref=dst, send_sem=send_sem.at[k], recv_sem=recv_sem.at[k],
            device_id=device, device_id_type=MESH,
        )

    def along(half, which, direction):
        step = 1 if direction == PLUS else -1
        on_x = (which == "f") == (half == 0)
        return at_x(step) if on_x else at_z(step)

    width = gate_w.shape[1]
    depth = gate_w.shape[0]
    part = depth // 2
    rows = SIDE * SIDE * CAP
    tokens = saved.shape[0]
    tile = min(256, width)
    half_rows = CAP // 2
    low_rows, high_rows = (0, half_rows), (half_rows, CAP)

    def gather_copies(table):
        made = {}
        for h in (0, 1):
            for d in (PLUS, MINUS):
                back = 2 if d == PLUS else 1
                rows_here = low_rows if d == PLUS else high_rows
                first = 0 if d == PLUS else 2
                f, s = along(h, "f", d), along(h, "s", d)
                made[h, d, "near"] = remote(group(table, h, (0, 1), 0), group(table, h, (back, back + 1), 0), f)
                made[h, d, "own"] = remote(group(table, h, (0, 1), 0), group(table, h, (0, 1), back), s)
                made[h, d, "far"] = remote(rows_of(table, h, back, rows_here), rows_of(table, h, 3, rows_here), f)
                made[h, d, "beside"] = remote(group(table, h, (1, 3), 0), group(table, h, (1, 3), back), s)
                made[h, d, "across"] = remote(group(table, h, (3, 4), 0), group(table, h, (3, 4), back), s)
                for name, p in (("pass_0", first), ("pass_1", first + 1)):
                    made[h, d, name] = remote(group(table, h, (p, p + 1), back), group(table, h, (p, p + 1), 3), s)
        return made

    def fin_slice(t, half, direction, pair):
        low, high = pair
        if half == 0:
            return fin_s0.at[t, direction, low:high]
        return fin_s1.at[t, direction, low * CAP : high * CAP]

    def acc_slice(t, half, direction, low):
        if half == 0:
            return acc_s0.at[t, direction, low : low + 1]
        return acc_s1.at[t, direction, low * CAP : (low + 1) * CAP]

    def scatter_copies(table, t):
        made = {}
        for h in (0, 1):
            acc = acc_s0 if h == 0 else acc_s1
            for d in (PLUS, MINUS):
                near = 1 if d == PLUS else 2
                mine, other = ((0, 2), (2, 4)) if d == PLUS else ((2, 4), (0, 2))
                my_rows, other_rows = (low_rows, high_rows) if d == PLUS else (high_rows, low_rows)
                f, s = along(h, "f", d), along(h, "s", d)
                made[h, d, "sa"] = remote(group(table, h, mine, 3), acc.at[t, d], s)
                made[h, d, "sd"] = remote(group(table, h, other, near), fin_slice(t, h, d, other), s)
                for name, p in (("sf_0", mine[0] + 1), ("sf_1", mine[0])):
                    made[h, d, name] = remote(group(table, h, (p, p + 1), near), fin_slice(t, h, d, (p, p + 1)), s)
                made[h, d, "fa"] = remote(rows_of(table, h, 3, my_rows), acc_f.at[t, h, d], f)
                made[h, d, "fd"] = remote(
                    rows_of(table, h, near, other_rows), fin_f.at[t, h, d, other_rows[0] : other_rows[1]], f
                )
                made[h, d, "ff"] = remote(
                    rows_of(table, h, near, my_rows), fin_f.at[t, h, d, my_rows[0] : my_rows[1]], f
                )
        return made

    both = [(h, d) for h in (0, 1) for d in (PLUS, MINUS)]
    copy_x = remote(x_in.at[0], x_here, at_section(1))
    copy_dy = remote(dy_in.at[0], cot, at_section(-1))
    gather_b, gather_c, gather_a = gather_copies(tab_b), gather_copies(tab_c), gather_copies(tab_a)
    scatter_b, scatter_a = scatter_copies(tab_b, 0), scatter_copies(tab_c, 1)

    def sent(copies):
        for copy in copies.values():
            copy.wait_send()

    def gather_0(copies):
        for name in ("near", "own"):
            for h, d in both:
                copies[h, d, name].start()

    def gather_1(copies):
        for h in (0, 1):
            for d in (PLUS, MINUS):
                copies[h, d, "near"].wait_recv()
                copies[h, d, "far"].start()
            for d in (PLUS, MINUS):
                copies[h, d, "beside"].start()

    def gather_2(copies):
        for h in (0, 1):
            for d in (PLUS, MINUS):
                copies[h, d, "far"].wait_recv()
            for d in (PLUS, MINUS):
                copies[h, d, "across"].start()
                copies[h, d, "own"].wait_recv()
            copies[h, PLUS, "pass_0"].start()

    def gather_3(copies):
        for h, d in both:
            copies[h, d, "beside"].wait_recv()
            copies[h, d, "pass_1" if d == PLUS else "pass_0"].start()

    def gather_4(copies):
        for h, d in both:
            copies[h, d, "across"].wait_recv()
            if d == MINUS:
                copies[h, d, "pass_1"].start()

    def gather_5(copies):
        for h, d in both:
            copies[h, d, "pass_0"].wait_recv()
            copies[h, d, "pass_1"].wait_recv()

    def scatter_0(copies, h):
        for name in ("sa", "sd"):
            for d in (PLUS, MINUS):
                copies[h, d, name].start()

    def add_into(target, other):
        target[...] = (target[...].astype(F32) + other[...].astype(F32)).astype(BF16)

    def scatter_1(copies, table, t):
        for h in (0, 1):
            for d in (PLUS, MINUS):
                copies[h, d, "sa"].wait_recv()
            for name, offset in (("sf_0", 1), ("sf_1", 0)):
                for d in (PLUS, MINUS):
                    near, p = (1, offset) if d == PLUS else (2, 2 + offset)
                    add_into(group(table, h, (p, p + 1), near), acc_slice(t, h, d, offset))
                    copies[h, d, name].start()

    def total(table, t, h, p):
        target = group(table, h, (p, p + 1), 0)
        one, two = fin_slice(t, h, PLUS, (p, p + 1)), fin_slice(t, h, MINUS, (p, p + 1))
        target[...] = (target[...].astype(F32) + one[...].astype(F32) + two[...].astype(F32)).astype(BF16)

    def scatter_2(copies, table, t):
        for h in (0, 1):
            for d in (PLUS, MINUS):
                copies[h, d, "sd"].wait_recv()
                copies[h, d, "sf_0"].wait_recv()
            total(table, t, h, 3)
            for d in (PLUS, MINUS):
                copies[h, d, "fa"].start()
            total(table, t, h, 1)
            copies[h, PLUS, "fd"].start()
        for h in (0, 1):
            copies[h, MINUS, "sf_1"].wait_recv()
            total(table, t, h, 2)
            copies[h, MINUS, "fd"].start()

    def scatter_3(copies, table, t):
        for h, d in both:
            near = 1 if d == PLUS else 2
            my_rows = low_rows if d == PLUS else high_rows
            copies[h, d, "fa"].wait_recv()
            add_into(rows_of(table, h, near, my_rows), acc_f.at[t, h, d])
            copies[h, d, "ff"].start()

    def scatter_own(copies, table, t):
        for h in (0, 1):
            copies[h, PLUS, "sf_1"].wait_recv()
            total(table, t, h, 0)

    def scatter_4(copies, table, t):
        for h in (0, 1):
            for d in (PLUS, MINUS):
                copies[h, d, "fd"].wait_recv()
                copies[h, d, "ff"].wait_recv()
            out = (
                rows_of(table, h, 0, (0, CAP))[...].astype(F32)
                + fin_f[t, h, PLUS].astype(F32)
                + fin_f[t, h, MINUS].astype(F32)
            )
            rows_out[t, :, h * part : (h + 1) * part] = out.astype(BF16)
            if t == 1:
                write_rows[h].start()

    barrier = pltpu.get_barrier_semaphore()
    for device in (at_x(1), at_x(-1), at_z(1), at_z(-1), at_section(1), at_section(-1)):
        pl.semaphore_signal(barrier, inc=1, device_id=device, device_id_type=MESH)
    small = [
        pltpu.make_async_copy(src, dst, small_sem.at[k])
        for k, (src, dst) in enumerate(
            ((ids_b_in, ids_b), (gates_b_in, gates_b), (ids_a_in, ids_a), (gates_a_in, gates_a), (gain_in, gain_ref))
        )
    ]
    quarter = tokens // 4
    load_saved = [
        pltpu.make_async_copy(x_saved.at[0, at], saved.at[at], local_sem.at[7 + k])
        for k, at in enumerate(pl.ds(k * quarter, quarter) for k in range(4))
    ]
    for copy in load_saved + small:
        copy.start()
    loads = [
        pltpu.make_async_copy(src.at[0], dst, local_sem.at[k])
        for k, (src, dst) in enumerate(((w_gate, gate_w), (w_up, up_w), (w_down, down_w)), start=1)
    ]
    keep_x = pltpu.make_async_copy(x_here, x_out, local_sem.at[6])
    write_rows = [
        pltpu.make_async_copy(rows_out.at[1, :, at], rows_a_out.at[:, at], local_sem.at[k])
        for k, at in ((0, pl.ds(0, part)), (5, pl.ds(part, part)))
    ]

    for copy in small:
        copy.wait()
    flag_a, share_a = flag_and_share(ids_a, gates_a)
    flag_b, share_b = flag_and_share(ids_b, gates_b)
    slot_rows = lax.broadcasted_iota(jnp.int32, (CAP, tokens), 0).astype(F32)
    slot_cols = lax.broadcasted_iota(jnp.int32, (tokens, CAP), 1).astype(F32)
    code_b = slot_code(flag_b)
    take_a = jnp.where(slot_code(flag_a) == slot_rows, 1.0, 0.0).astype(BF16)
    take_b = jnp.where(code_b == slot_rows, 1.0, 0.0)
    share_slot = jnp.sum(take_b * share_b, axis=1, keepdims=True)
    take_b = take_b.astype(BF16)
    place_b[...] = jnp.where(column(code_b) == slot_cols, 1.0, 0.0).astype(BF16)


    def put_own(table, values):
        for h in (0, 1):
            table[h, 0, 0:CAP, :] = values[:, h * part : (h + 1) * part]

    def normed(values):
        scale = lax.rsqrt(jnp.mean(values * values, axis=-1, keepdims=True) + EPSILON)
        return (values * scale * gain_ref[...]).astype(BF16)

    for copy in load_saved:
        copy.wait()
    put_own(tab_b, normed(dot(take_b, saved[...])))
    def rows_c():
        copy_dy.wait_recv()
        put_own(tab_c, (share_slot * dot(take_b, cot[...])).astype(BF16))

    def rows_a():
        copy_x.wait_recv()
        keep_x.start()
        put_own(tab_a, normed(dot(take_a, x_here[...])))

    gather = (gather_0, gather_1, gather_2, gather_3, gather_4, gather_5)
    steps = {"dy": rows_c, "x": rows_a}
    for name, copies in (("a", gather_a), ("b", gather_b), ("c", gather_c)):
        for k, step in enumerate(gather):
            steps[f"{name}{k}"] = functools.partial(step, copies)
    scatter = {1: scatter_1, 2: scatter_2, 3: scatter_3, 4: scatter_4, 5: scatter_own}
    for name, copies, table, t in (("a", scatter_a, tab_c, 1), ("b", scatter_b, tab_b, 0)):
        for k, step in scatter.items():
            steps[f"s{name}{k}"] = functools.partial(step, copies, table, t)

    def do(*names):
        for name in names:
            steps[name]()

    def during(label, i):
        for k, names in PLAN[label].items():

            @pl.when(i == k)
            def _():
                do(*names)

    pl.semaphore_wait(barrier, 6)
    copy_x.start()
    copy_dy.start()
    do("b0")
    for load in loads:
        load.start()
    do(*PLAN["early"])
    for load in loads:
        load.wait()

    def tall(table, h):
        return table[h].reshape(rows, part)

    def strip(i, size):
        return pl.ds(pl.multiple_of(i * size, size), size)

    def columns(i):
        return strip(i, tile)

    def project(table, weight, i):
        return dot(tall(table, 0), weight[0:part, columns(i)]) + dot(tall(table, 1), weight[part:depth, columns(i)])

    count = width // tile

    @pl.loop(0, count)
    def _(i):
        gate_b[:, columns(i)] = project(tab_b, gate_w, i)
        up_b[:, columns(i)] = project(tab_b, up_w, i)
        during("project b", i)

    do(*PLAN["before hidden"])

    @pl.loop(0, 2)
    def _(i):
        at = strip(i, width // 2)
        hidden_grad = dot_nt(tall(tab_c, 0), down_w[at, 0:part]) + dot_nt(tall(tab_c, 1), down_w[at, part:depth])
        gate = gate_b[:, at]
        sigmoid = jax.nn.sigmoid(gate)
        gate_g[:, at] = (hidden_grad * up_b[:, at] * (sigmoid * (1.0 + gate * (1.0 - sigmoid)))).astype(BF16)
        up_g[:, at] = (hidden_grad * (gate * sigmoid)).astype(BF16)
        during("hidden grad", i)

    sent(gather_b)
    for h in (0, 1):

        @pl.loop(0, 2)
        def _(i):
            at = strip(2 * h + i, part // 2)
            back = dot_nt(gate_g[...], gate_w[at, :]) + dot_nt(up_g[...], up_w[at, :])
            tab_b[h, :, :, strip(i, part // 2)] = back.astype(BF16).reshape(SIDE, SIDE * CAP, part // 2)
            during(f"back {h}", i)

        scatter_0(scatter_b, h)

    do(*PLAN["before project a"])

    @pl.loop(0, count)
    def _(i):
        gate = project(tab_a, gate_w, i)
        up = project(tab_a, up_w, i)
        hidden[:, columns(i)] = (gate * jax.nn.sigmoid(gate) * up).astype(BF16)
        during("project a", i)

    sent(gather_c)
    for h in (0, 1):

        @pl.loop(0, 2)
        def _(i):
            at = strip(2 * h + i, part // 2)
            out = dot(hidden[...], down_w[:, at])
            tab_c[h, :, :, strip(i, part // 2)] = out.astype(BF16).reshape(SIDE, SIDE * CAP, part // 2)
            during(f"down {h}", i)

        scatter_0(scatter_a, h)

    scatter_2(scatter_b, tab_b, 0)
    scatter_1(scatter_a, tab_c, 1)
    scatter_3(scatter_b, tab_b, 0)
    scatter_own(scatter_b, tab_b, 0)
    scatter_2(scatter_a, tab_c, 1)
    scatter_4(scatter_b, tab_b, 0)

    chunk = tokens // 4

    def grad_part(i):
        at = pl.ds(pl.multiple_of(i * chunk, chunk), chunk)
        values = saved[at, :].astype(F32)
        scale = lax.rsqrt(jnp.mean(values * values, axis=-1, keepdims=True) + EPSILON)
        weighted = dot(place_b[at, :], rows_out[0]) * gain_ref[...]
        average = jnp.mean(weighted * values, axis=-1, keepdims=True)
        grad = cot[at, :].astype(F32) + scale * (weighted - values * scale * scale * average)
        cot[at, :] = grad.astype(BF16)

    scatter_3(scatter_a, tab_c, 1)
    pl.loop(0, 4)(grad_part)
    write_grad = pltpu.make_async_copy(cot, grad_out, local_sem.at[4])
    write_grad.start()
    scatter_own(scatter_a, tab_c, 1)
    scatter_4(scatter_a, tab_c, 1)
    sent(gather_a)
    sent(scatter_b)
    sent(scatter_a)
    copy_x.wait_send()
    copy_dy.wait_send()
    keep_x.wait()
    write_grad.wait()
    for copy in write_rows:
        copy.wait()


def finish(ids_in, gates_in, x_here, rows_a, grad, mixed_out, grad_out, ids_a, gates_a, x_part, grad_part, rows, sem):
    tokens = x_part.shape[0]
    chunk = tokens // 4
    load_rows = pltpu.make_async_copy(rows_a, rows, sem.at[8])
    load_ids = pltpu.make_async_copy(ids_in, ids_a, sem.at[17])
    load_gates = pltpu.make_async_copy(gates_in, gates_a, sem.at[18])
    for copy in (load_ids, load_gates, load_rows):
        copy.start()
    chunks = [pl.ds(i * chunk, chunk) for i in range(4)]
    wide = x_part.shape[1] // 4
    strips = [pl.ds(i * wide, wide) for i in range(4)]
    loads = [pltpu.make_async_copy(x_here.at[:, at], x_part.at[:, at], sem.at[i]) for i, at in enumerate(strips)]
    takes = [pltpu.make_async_copy(grad.at[at], grad_part.at[at], sem.at[4 + i]) for i, at in enumerate(chunks)]
    for copy in loads + takes:
        copy.start()
    load_ids.wait()
    load_gates.wait()
    flag, share = flag_and_share(ids_a, gates_a)
    place = (column(slot_code(flag)) == lax.broadcasted_iota(jnp.int32, (tokens, CAP), 1).astype(F32)).astype(F32)
    place = place.astype(BF16)
    share = column(share)
    load_rows.wait()
    writes = []
    for i, (at, strip) in enumerate(zip(chunks, strips)):
        loads[i].wait()
        x_part[:, strip] = (x_part[:, strip].astype(F32) + share * dot(place, rows[:, strip])).astype(BF16)
        writes.append(pltpu.make_async_copy(x_part.at[:, strip], mixed_out.at[0, :, strip], sem.at[9 + i]))
        writes[-1].start()
        takes[i].wait()
        writes.append(pltpu.make_async_copy(grad_part.at[at], grad_out.at[0, at], sem.at[13 + i]))
        writes[-1].start()
    for write in writes:
        write.wait()


def shards(sections, x_in, ids_a, gates_a, x_saved, ids_b, gates_b, dy_in, gain, w_gate, w_up, w_down):
    _, tokens, depth = x_in.shape
    width = w_gate.shape[2]
    rows, part = SIDE * SIDE * CAP, depth // 2
    copies = 2 + 3 * 28 + 2 * 28
    table = pltpu.VMEM((2, SIDE, SIDE * CAP, part), BF16)
    flops = 8 * 2 * rows * depth * width
    anywhere = pl.BlockSpec(memory_space=pl.ANY)
    block = jax.ShapeDtypeStruct((tokens, depth), BF16)
    routes = ids_a[0].T, gates_a[0].T, ids_b[0].T, gates_b[0].T
    x_here, grad, rows_a = pl.pallas_call(
        functools.partial(kernel, sections),
        out_shape=[block, block, jax.ShapeDtypeStruct((CAP, depth), BF16)],
        in_specs=[anywhere] * 11,
        out_specs=[anywhere] * 3,
        scratch_shapes=[
            pltpu.VMEM((depth, width), BF16),
            pltpu.VMEM((depth, width), BF16),
            pltpu.VMEM((width, depth), BF16),
            table, table, table,
            pltpu.VMEM((rows, width), F32),
            pltpu.VMEM((rows, width), F32),
            pltpu.VMEM((rows, width), BF16),
            pltpu.VMEM((rows, width), BF16),
            pltpu.VMEM((rows, width), BF16),
            pltpu.VMEM((tokens, depth), BF16),
            pltpu.VMEM((tokens, depth), BF16),
            pltpu.VMEM((tokens, depth), BF16),
            pltpu.VMEM((2, 2, 2, CAP, part), BF16),
            pltpu.VMEM((2, 2, 2 * CAP, part), BF16),
            pltpu.VMEM((2, 2, SIDE, CAP, part), BF16),
            pltpu.VMEM((2, 2, SIDE * CAP, part), BF16),
            pltpu.VMEM((2, 2, 2, CAP // 2, part), BF16),
            pltpu.VMEM((2, 2, 2, CAP, part), BF16),
            pltpu.VMEM((tokens, CAP), BF16),
            pltpu.VMEM((2, CAP, depth), BF16),
            pltpu.VMEM((2, tokens), jnp.int32),
            pltpu.VMEM((2, tokens), F32),
            pltpu.VMEM((2, tokens), jnp.int32),
            pltpu.VMEM((2, tokens), F32),
            pltpu.VMEM((1, depth), F32),
            pltpu.SemaphoreType.DMA((copies,)),
            pltpu.SemaphoreType.DMA((copies,)),
            pltpu.SemaphoreType.DMA((11,)),
            pltpu.SemaphoreType.DMA((5,)),
        ],
        compiler_params=pltpu.CompilerParams(
            collective_id=0, has_side_effects=True, vmem_limit_bytes=60 * 1024 * 1024
        ),
        cost_estimate=pl.CostEstimate(
            flops=flops, bytes_accessed=3 * depth * width * 2 + 5 * tokens * depth * 2, transcendentals=2 * rows * width
        ),
    )(*routes, gain, x_in, x_saved, dy_in, w_gate, w_up, w_down)
    return pl.pallas_call(
        finish,
        out_shape=[jax.ShapeDtypeStruct(x_in.shape, BF16)] * 2,
        in_specs=[anywhere] * 5,
        out_specs=[anywhere] * 2,
        scratch_shapes=[
            pltpu.VMEM((2, tokens), jnp.int32),
            pltpu.VMEM((2, tokens), F32),
            pltpu.VMEM((tokens, depth), BF16),
            pltpu.VMEM((tokens, depth), BF16),
            pltpu.VMEM((CAP, depth), BF16),
            pltpu.SemaphoreType.DMA((19,)),
        ],
        compiler_params=pltpu.CompilerParams(vmem_limit_bytes=60 * 1024 * 1024),
    )(routes[0], routes[1], x_here, rows_a, grad)


def solution(mesh):
    tokens = P("section", "ed", None)
    return jax.shard_map(
        functools.partial(shards, mesh.shape["section"]),
        mesh=mesh,
        in_specs=(tokens,) * 7
        + (P("section", None), P("section", None, "ed"), P("section", None, "ed"), P("section", "ed", None)),
        out_specs=(tokens, tokens),
        check_vma=False,
    )
```

```python
import functools

import jax
import jax.numpy as jnp
from jax import lax
from jax.experimental import pallas as pl
from jax.experimental.pallas import tpu as pltpu
from jax.sharding import PartitionSpec as P

EPSILON = 1e-06
MESH = pl.DeviceIdType.MESH
SIDE = 4
CAP = 32
PLUS, MINUS = 0, 1
PLAN = {
    "early": ("b1", "b2", "dy", "c0", "b3", "c1", "b4", "c2", "x", "b5", "c3", "a0", "c4"),
    "project b": {0: ("a1",)},
    "before hidden": ("c5",),
    "hidden grad": {0: ("a2",), 1: ("a3",)},
    "back 0": {0: ("a4",)},
    "back 1": {},
    "before project a": ("a5",),
    "project a": {1: ("sb1",)},
    "down 0": {},
    "down 1": {},
}
F32, BF16 = jnp.float32, jnp.bfloat16
NT = (((1,), (1,)), ((), ()))


def dot(a, b):
    return jnp.dot(a, b, preferred_element_type=F32)


def dot_nt(a, b):
    return lax.dot_general(a, b, NT, preferred_element_type=F32)


def group(table, half, first, second):
    low, high = first
    if half == 0:
        return table.at[0, low:high, second * CAP : (second + 1) * CAP]
    return table.at[1, second, low * CAP : high * CAP]


def rows_of(table, half, first, rows):
    low, high = rows
    if half == 0:
        return table.at[0, first, low:high]
    return table.at[1, 0, first * CAP + low : first * CAP + high]


def flag_and_share(ids, gates):
    chosen = ids[...] == 0
    return (
        jnp.sum(jnp.where(chosen, 1.0, 0.0), axis=0, keepdims=True),
        jnp.sum(jnp.where(chosen, gates[...], 0.0), axis=0, keepdims=True),
    )


def column(row):
    n = row.shape[1]
    rows, columns = lax.broadcasted_iota(jnp.int32, (n, n), 0), lax.broadcasted_iota(jnp.int32, (n, n), 1)
    return jnp.sum(jnp.where(rows == columns, row, 0.0), axis=1, keepdims=True)


def slot_code(flag):
    n = flag.shape[1]
    rows, columns = lax.broadcasted_iota(jnp.int32, (n, n), 0), lax.broadcasted_iota(jnp.int32, (n, n), 1)
    count = jnp.sum(jnp.where(rows <= columns, column(flag), 0.0), axis=0, keepdims=True)
    return jnp.where(flag > 0.5, count - 1.0, -1.0)


def kernel(
    sections,
    ids_a_in, gates_a_in, ids_b_in, gates_b_in, gain_in, x_in, x_saved, dy_in, w_gate, w_up, w_down,
    x_out, grad_out, rows_a_out,
    gate_w, up_w, down_w, tab_b, tab_c, tab_a,
    gate_b, up_b, gate_g, up_g, hidden,
    x_here, saved, cot,
    acc_s0, acc_s1, fin_s0, fin_s1, acc_f, fin_f,
    place_b, rows_out, ids_a, gates_a, ids_b, gates_b, gain_ref,
    send_sem, recv_sem, local_sem, small_sem,
):
    section, ed = lax.axis_index("section"), lax.axis_index("ed")
    x, z = ed // SIDE, ed % SIDE

    def at_x(step):
        return (section, (x + step + SIDE) % SIDE * SIDE + z)

    def at_z(step):
        return (section, x * SIDE + (z + step + SIDE) % SIDE)

    def at_section(step):
        return ((section + step + sections) % sections, ed)

    counter = [0]

    def remote(src, dst, device):
        k = counter[0]
        counter[0] += 1
        return pltpu.make_async_remote_copy(
            src_ref=src, dst_ref=dst, send_sem=send_sem.at[k], recv_sem=recv_sem.at[k],
            device_id=device, device_id_type=MESH,
        )

    def along(half, which, direction):
        step = 1 if direction == PLUS else -1
        on_x = (which == "f") == (half == 0)
        return at_x(step) if on_x else at_z(step)

    width = gate_w.shape[1]
    depth = gate_w.shape[0]
    part = depth // 2
    rows = SIDE * SIDE * CAP
    tokens = saved.shape[0]
    tile = min(256, width)
    half_rows = CAP // 2
    low_rows, high_rows = (0, half_rows), (half_rows, CAP)

    def gather_copies(table):
        made = {}
        for h in (0, 1):
            for d in (PLUS, MINUS):
                back = 2 if d == PLUS else 1
                rows_here = low_rows if d == PLUS else high_rows
                first = 0 if d == PLUS else 2
                f, s = along(h, "f", d), along(h, "s", d)
                made[h, d, "near"] = remote(group(table, h, (0, 1), 0), group(table, h, (back, back + 1), 0), f)
                made[h, d, "own"] = remote(group(table, h, (0, 1), 0), group(table, h, (0, 1), back), s)
                made[h, d, "far"] = remote(rows_of(table, h, back, rows_here), rows_of(table, h, 3, rows_here), f)
                made[h, d, "beside"] = remote(group(table, h, (1, 3), 0), group(table, h, (1, 3), back), s)
                made[h, d, "across"] = remote(group(table, h, (3, 4), 0), group(table, h, (3, 4), back), s)
                for name, p in (("pass_0", first), ("pass_1", first + 1)):
                    made[h, d, name] = remote(group(table, h, (p, p + 1), back), group(table, h, (p, p + 1), 3), s)
        return made

    def fin_slice(t, half, direction, pair):
        low, high = pair
        if half == 0:
            return fin_s0.at[t, direction, low:high]
        return fin_s1.at[t, direction, low * CAP : high * CAP]

    def acc_slice(t, half, direction, low):
        if half == 0:
            return acc_s0.at[t, direction, low : low + 1]
        return acc_s1.at[t, direction, low * CAP : (low + 1) * CAP]

    def scatter_copies(table, t):
        made = {}
        for h in (0, 1):
            acc = acc_s0 if h == 0 else acc_s1
            for d in (PLUS, MINUS):
                near = 1 if d == PLUS else 2
                mine, other = ((0, 2), (2, 4)) if d == PLUS else ((2, 4), (0, 2))
                my_rows, other_rows = (low_rows, high_rows) if d == PLUS else (high_rows, low_rows)
                f, s = along(h, "f", d), along(h, "s", d)
                made[h, d, "sa"] = remote(group(table, h, mine, 3), acc.at[t, d], s)
                made[h, d, "sd"] = remote(group(table, h, other, near), fin_slice(t, h, d, other), s)
                for name, p in (("sf_0", mine[0] + 1), ("sf_1", mine[0])):
                    made[h, d, name] = remote(group(table, h, (p, p + 1), near), fin_slice(t, h, d, (p, p + 1)), s)
                made[h, d, "fa"] = remote(rows_of(table, h, 3, my_rows), acc_f.at[t, h, d], f)
                made[h, d, "fd"] = remote(
                    rows_of(table, h, near, other_rows), fin_f.at[t, h, d, other_rows[0] : other_rows[1]], f
                )
                made[h, d, "ff"] = remote(
                    rows_of(table, h, near, my_rows), fin_f.at[t, h, d, my_rows[0] : my_rows[1]], f
                )
        return made

    both = [(h, d) for h in (0, 1) for d in (PLUS, MINUS)]
    copy_x = remote(x_in.at[0], x_here, at_section(1))
    copy_dy = remote(dy_in.at[0], cot, at_section(-1))
    gather_b, gather_c, gather_a = gather_copies(tab_b), gather_copies(tab_c), gather_copies(tab_a)
    scatter_b, scatter_a = scatter_copies(tab_b, 0), scatter_copies(tab_c, 1)

    def sent(copies):
        for copy in copies.values():
            copy.wait_send()

    def gather_0(copies):
        for name in ("near", "own"):
            for h, d in both:
                copies[h, d, name].start()

    def gather_1(copies):
        for h in (0, 1):
            for d in (PLUS, MINUS):
                copies[h, d, "near"].wait_recv()
                copies[h, d, "far"].start()
            for d in (PLUS, MINUS):
                copies[h, d, "beside"].start()

    def gather_2(copies):
        for h in (0, 1):
            for d in (PLUS, MINUS):
                copies[h, d, "far"].wait_recv()
            for d in (PLUS, MINUS):
                copies[h, d, "across"].start()
                copies[h, d, "own"].wait_recv()
            copies[h, PLUS, "pass_0"].start()

    def gather_3(copies):
        for h, d in both:
            copies[h, d, "beside"].wait_recv()
            copies[h, d, "pass_1" if d == PLUS else "pass_0"].start()

    def gather_4(copies):
        for h, d in both:
            copies[h, d, "across"].wait_recv()
            if d == MINUS:
                copies[h, d, "pass_1"].start()

    def gather_5(copies):
        for h, d in both:
            copies[h, d, "pass_0"].wait_recv()
            copies[h, d, "pass_1"].wait_recv()

    def scatter_0(copies, h):
        for name in ("sa", "sd"):
            for d in (PLUS, MINUS):
                copies[h, d, name].start()

    def add_into(target, other):
        target[...] = (target[...].astype(F32) + other[...].astype(F32)).astype(BF16)

    def scatter_1(copies, table, t):
        for h in (0, 1):
            for d in (PLUS, MINUS):
                copies[h, d, "sa"].wait_recv()
            for name, offset in (("sf_0", 1), ("sf_1", 0)):
                for d in (PLUS, MINUS):
                    near, p = (1, offset) if d == PLUS else (2, 2 + offset)
                    add_into(group(table, h, (p, p + 1), near), acc_slice(t, h, d, offset))
                    copies[h, d, name].start()

    def total(table, t, h, p):
        target = group(table, h, (p, p + 1), 0)
        one, two = fin_slice(t, h, PLUS, (p, p + 1)), fin_slice(t, h, MINUS, (p, p + 1))
        target[...] = (target[...].astype(F32) + one[...].astype(F32) + two[...].astype(F32)).astype(BF16)

    def scatter_2(copies, table, t):
        for h in (0, 1):
            for d in (PLUS, MINUS):
                copies[h, d, "sd"].wait_recv()
                copies[h, d, "sf_0"].wait_recv()
            total(table, t, h, 3)
            for d in (PLUS, MINUS):
                copies[h, d, "fa"].start()
            total(table, t, h, 1)
            copies[h, PLUS, "fd"].start()
        for h in (0, 1):
            copies[h, MINUS, "sf_1"].wait_recv()
            total(table, t, h, 2)
            copies[h, MINUS, "fd"].start()

    def scatter_3(copies, table, t):
        for h, d in both:
            near = 1 if d == PLUS else 2
            my_rows = low_rows if d == PLUS else high_rows
            copies[h, d, "fa"].wait_recv()
            add_into(rows_of(table, h, near, my_rows), acc_f.at[t, h, d])
            copies[h, d, "ff"].start()

    def scatter_own(copies, table, t):
        for h in (0, 1):
            copies[h, PLUS, "sf_1"].wait_recv()
            total(table, t, h, 0)

    def scatter_4(copies, table, t):
        for h in (0, 1):
            for d in (PLUS, MINUS):
                copies[h, d, "fd"].wait_recv()
                copies[h, d, "ff"].wait_recv()
            out = (
                rows_of(table, h, 0, (0, CAP))[...].astype(F32)
                + fin_f[t, h, PLUS].astype(F32)
                + fin_f[t, h, MINUS].astype(F32)
            )
            rows_out[t, :, h * part : (h + 1) * part] = out.astype(BF16)
            if t == 1:
                write_rows[h].start()

    barrier = pltpu.get_barrier_semaphore()
    for device in (at_x(1), at_x(-1), at_z(1), at_z(-1), at_section(1), at_section(-1)):
        pl.semaphore_signal(barrier, inc=1, device_id=device, device_id_type=MESH)
    small = [
        pltpu.make_async_copy(src, dst, small_sem.at[k])
        for k, (src, dst) in enumerate(
            ((ids_b_in, ids_b), (gates_b_in, gates_b), (ids_a_in, ids_a), (gates_a_in, gates_a), (gain_in, gain_ref))
        )
    ]
    quarter = tokens // 4
    load_saved = [
        pltpu.make_async_copy(x_saved.at[0, at], saved.at[at], local_sem.at[7 + k])
        for k, at in enumerate(pl.ds(k * quarter, quarter) for k in range(4))
    ]
    for copy in load_saved + small:
        copy.start()
    loads = [
        pltpu.make_async_copy(src.at[0], dst, local_sem.at[k])
        for k, (src, dst) in enumerate(((w_gate, gate_w), (w_up, up_w), (w_down, down_w)), start=1)
    ]
    keep_x = pltpu.make_async_copy(x_here, x_out, local_sem.at[6])
    write_rows = [
        pltpu.make_async_copy(rows_out.at[1, :, at], rows_a_out.at[:, at], local_sem.at[k])
        for k, at in ((0, pl.ds(0, part)), (5, pl.ds(part, part)))
    ]

    for copy in small:
        copy.wait()
    flag_a, share_a = flag_and_share(ids_a, gates_a)
    flag_b, share_b = flag_and_share(ids_b, gates_b)
    slot_rows = lax.broadcasted_iota(jnp.int32, (CAP, tokens), 0).astype(F32)
    slot_cols = lax.broadcasted_iota(jnp.int32, (tokens, CAP), 1).astype(F32)
    code_b = slot_code(flag_b)
    take_a = jnp.where(slot_code(flag_a) == slot_rows, 1.0, 0.0).astype(BF16)
    take_b = jnp.where(code_b == slot_rows, 1.0, 0.0)
    share_slot = jnp.sum(take_b * share_b, axis=1, keepdims=True)
    take_b = take_b.astype(BF16)
    place_b[...] = jnp.where(column(code_b) == slot_cols, 1.0, 0.0).astype(BF16)


    def put_own(table, values):
        for h in (0, 1):
            table[h, 0, 0:CAP, :] = values[:, h * part : (h + 1) * part]

    def normed(values):
        scale = lax.rsqrt(jnp.mean(values * values, axis=-1, keepdims=True) + EPSILON)
        return (values * scale * gain_ref[...]).astype(BF16)

    for copy in load_saved:
        copy.wait()
    put_own(tab_b, normed(dot(take_b, saved[...])))
    def rows_c():
        copy_dy.wait_recv()
        put_own(tab_c, (share_slot * dot(take_b, cot[...])).astype(BF16))

    def rows_a():
        copy_x.wait_recv()
        keep_x.start()
        put_own(tab_a, normed(dot(take_a, x_here[...])))

    gather = (gather_0, gather_1, gather_2, gather_3, gather_4, gather_5)
    steps = {"dy": rows_c, "x": rows_a}
    for name, copies in (("a", gather_a), ("b", gather_b), ("c", gather_c)):
        for k, step in enumerate(gather):
            steps[f"{name}{k}"] = functools.partial(step, copies)
    scatter = {1: scatter_1, 2: scatter_2, 3: scatter_3, 4: scatter_4, 5: scatter_own}
    for name, copies, table, t in (("a", scatter_a, tab_c, 1), ("b", scatter_b, tab_b, 0)):
        for k, step in scatter.items():
            steps[f"s{name}{k}"] = functools.partial(step, copies, table, t)

    def do(*names):
        for name in names:
            steps[name]()

    def during(label, i):
        for k, names in PLAN[label].items():

            @pl.when(i == k)
            def _():
                do(*names)

    pl.semaphore_wait(barrier, 6)
    copy_x.start()
    copy_dy.start()
    do("b0")
    for load in loads:
        load.start()
    do(*PLAN["early"])
    for load in loads:
        load.wait()

    def tall(table, h):
        return table[h].reshape(rows, part)

    def strip(i, size):
        return pl.ds(pl.multiple_of(i * size, size), size)

    def columns(i):
        return strip(i, tile)

    def project(table, weight, i):
        return dot(tall(table, 0), weight[0:part, columns(i)]) + dot(tall(table, 1), weight[part:depth, columns(i)])

    count = width // tile

    @pl.loop(0, count)
    def _(i):
        gate_b[:, columns(i)] = project(tab_b, gate_w, i)
        up_b[:, columns(i)] = project(tab_b, up_w, i)
        during("project b", i)

    do(*PLAN["before hidden"])

    @pl.loop(0, 2)
    def _(i):
        at = strip(i, width // 2)
        hidden_grad = dot_nt(tall(tab_c, 0), down_w[at, 0:part]) + dot_nt(tall(tab_c, 1), down_w[at, part:depth])
        gate = gate_b[:, at]
        sigmoid = jax.nn.sigmoid(gate)
        gate_g[:, at] = (hidden_grad * up_b[:, at] * (sigmoid * (1.0 + gate * (1.0 - sigmoid)))).astype(BF16)
        up_g[:, at] = (hidden_grad * (gate * sigmoid)).astype(BF16)
        during("hidden grad", i)

    sent(gather_b)
    for h in (0, 1):

        @pl.loop(0, 2)
        def _(i):
            at = strip(2 * h + i, part // 2)
            back = dot_nt(gate_g[...], gate_w[at, :]) + dot_nt(up_g[...], up_w[at, :])
            tab_b[h, :, :, strip(i, part // 2)] = back.astype(BF16).reshape(SIDE, SIDE * CAP, part // 2)
            during(f"back {h}", i)

        scatter_0(scatter_b, h)

    do(*PLAN["before project a"])

    @pl.loop(0, count)
    def _(i):
        gate = project(tab_a, gate_w, i)
        up = project(tab_a, up_w, i)
        hidden[:, columns(i)] = (gate * jax.nn.sigmoid(gate) * up).astype(BF16)
        during("project a", i)

    sent(gather_c)
    for h in (0, 1):

        @pl.loop(0, 2)
        def _(i):
            at = strip(2 * h + i, part // 2)
            out = dot(hidden[...], down_w[:, at])
            tab_c[h, :, :, strip(i, part // 2)] = out.astype(BF16).reshape(SIDE, SIDE * CAP, part // 2)
            during(f"down {h}", i)

        scatter_0(scatter_a, h)

    scatter_2(scatter_b, tab_b, 0)
    scatter_1(scatter_a, tab_c, 1)
    scatter_3(scatter_b, tab_b, 0)
    scatter_own(scatter_b, tab_b, 0)
    scatter_2(scatter_a, tab_c, 1)
    scatter_4(scatter_b, tab_b, 0)

    chunk = tokens // 4

    def grad_part(i):
        at = pl.ds(pl.multiple_of(i * chunk, chunk), chunk)
        values = saved[at, :].astype(F32)
        scale = lax.rsqrt(jnp.mean(values * values, axis=-1, keepdims=True) + EPSILON)
        weighted = dot(place_b[at, :], rows_out[0]) * gain_ref[...]
        average = jnp.mean(weighted * values, axis=-1, keepdims=True)
        grad = cot[at, :].astype(F32) + scale * (weighted - values * scale * scale * average)
        cot[at, :] = grad.astype(BF16)

    scatter_3(scatter_a, tab_c, 1)
    pl.loop(0, 4)(grad_part)
    write_grad = pltpu.make_async_copy(cot, grad_out, local_sem.at[4])
    write_grad.start()
    scatter_own(scatter_a, tab_c, 1)
    scatter_4(scatter_a, tab_c, 1)
    sent(gather_a)
    sent(scatter_b)
    sent(scatter_a)
    copy_x.wait_send()
    copy_dy.wait_send()
    keep_x.wait()
    write_grad.wait()
    for copy in write_rows:
        copy.wait()


def finish(ids_in, gates_in, x_here, rows_a, grad, mixed_out, grad_out, ids_a, gates_a, x_part, grad_part, rows, sem):
    tokens = x_part.shape[0]
    pieces = 8
    chunk = tokens // pieces
    load_ids = pltpu.make_async_copy(ids_in, ids_a, sem.at[40])
    load_gates = pltpu.make_async_copy(gates_in, gates_a, sem.at[41])
    for copy in (load_ids, load_gates):
        copy.start()
    chunks = [pl.ds(i * chunk, chunk) for i in range(pieces)]
    wide = x_part.shape[1] // pieces
    strips = [pl.ds(i * wide, wide) for i in range(pieces)]
    load_rows = [pltpu.make_async_copy(rows_a.at[:, at], rows.at[:, at], sem.at[16 + i]) for i, at in enumerate(strips)]
    loads = [pltpu.make_async_copy(x_here.at[:, at], x_part.at[:, at], sem.at[i]) for i, at in enumerate(strips)]
    takes = [pltpu.make_async_copy(grad.at[at], grad_part.at[at], sem.at[8 + i]) for i, at in enumerate(chunks)]
    for i in range(pieces):
        load_rows[i].start()
        loads[i].start()
    for copy in takes:
        copy.start()
    load_ids.wait()
    load_gates.wait()
    flag, share = flag_and_share(ids_a, gates_a)
    place = (column(slot_code(flag)) == lax.broadcasted_iota(jnp.int32, (tokens, CAP), 1).astype(F32)).astype(F32)
    place = place.astype(BF16)
    share = column(share)
    writes = []
    for i, (at, strip) in enumerate(zip(chunks, strips)):
        load_rows[i].wait()
        loads[i].wait()
        x_part[:, strip] = (x_part[:, strip].astype(F32) + share * dot(place, rows[:, strip])).astype(BF16)
        writes.append(pltpu.make_async_copy(x_part.at[:, strip], mixed_out.at[0, :, strip], sem.at[24 + i]))
        writes[-1].start()
        takes[i].wait()
        writes.append(pltpu.make_async_copy(grad_part.at[at], grad_out.at[0, at], sem.at[32 + i]))
        writes[-1].start()
    for write in writes:
        write.wait()


def shards(sections, x_in, ids_a, gates_a, x_saved, ids_b, gates_b, dy_in, gain, w_gate, w_up, w_down):
    _, tokens, depth = x_in.shape
    width = w_gate.shape[2]
    rows, part = SIDE * SIDE * CAP, depth // 2
    copies = 2 + 3 * 28 + 2 * 28
    table = pltpu.VMEM((2, SIDE, SIDE * CAP, part), BF16)
    flops = 8 * 2 * rows * depth * width
    anywhere = pl.BlockSpec(memory_space=pl.ANY)
    block = jax.ShapeDtypeStruct((tokens, depth), BF16)
    routes = ids_a[0].T, gates_a[0].T, ids_b[0].T, gates_b[0].T
    x_here, grad, rows_a = pl.pallas_call(
        functools.partial(kernel, sections),
        out_shape=[block, block, jax.ShapeDtypeStruct((CAP, depth), BF16)],
        in_specs=[anywhere] * 11,
        out_specs=[anywhere] * 3,
        scratch_shapes=[
            pltpu.VMEM((depth, width), BF16),
            pltpu.VMEM((depth, width), BF16),
            pltpu.VMEM((width, depth), BF16),
            table, table, table,
            pltpu.VMEM((rows, width), F32),
            pltpu.VMEM((rows, width), F32),
            pltpu.VMEM((rows, width), BF16),
            pltpu.VMEM((rows, width), BF16),
            pltpu.VMEM((rows, width), BF16),
            pltpu.VMEM((tokens, depth), BF16),
            pltpu.VMEM((tokens, depth), BF16),
            pltpu.VMEM((tokens, depth), BF16),
            pltpu.VMEM((2, 2, 2, CAP, part), BF16),
            pltpu.VMEM((2, 2, 2 * CAP, part), BF16),
            pltpu.VMEM((2, 2, SIDE, CAP, part), BF16),
            pltpu.VMEM((2, 2, SIDE * CAP, part), BF16),
            pltpu.VMEM((2, 2, 2, CAP // 2, part), BF16),
            pltpu.VMEM((2, 2, 2, CAP, part), BF16),
            pltpu.VMEM((tokens, CAP), BF16),
            pltpu.VMEM((2, CAP, depth), BF16),
            pltpu.VMEM((2, tokens), jnp.int32),
            pltpu.VMEM((2, tokens), F32),
            pltpu.VMEM((2, tokens), jnp.int32),
            pltpu.VMEM((2, tokens), F32),
            pltpu.VMEM((1, depth), F32),
            pltpu.SemaphoreType.DMA((copies,)),
            pltpu.SemaphoreType.DMA((copies,)),
            pltpu.SemaphoreType.DMA((11,)),
            pltpu.SemaphoreType.DMA((5,)),
        ],
        compiler_params=pltpu.CompilerParams(
            collective_id=0, has_side_effects=True, vmem_limit_bytes=60 * 1024 * 1024
        ),
        cost_estimate=pl.CostEstimate(
            flops=flops, bytes_accessed=3 * depth * width * 2 + 5 * tokens * depth * 2, transcendentals=2 * rows * width
        ),
    )(*routes, gain, x_in, x_saved, dy_in, w_gate, w_up, w_down)
    return pl.pallas_call(
        finish,
        out_shape=[jax.ShapeDtypeStruct(x_in.shape, BF16)] * 2,
        in_specs=[anywhere] * 5,
        out_specs=[anywhere] * 2,
        scratch_shapes=[
            pltpu.VMEM((2, tokens), jnp.int32),
            pltpu.VMEM((2, tokens), F32),
            pltpu.VMEM((tokens, depth), BF16),
            pltpu.VMEM((tokens, depth), BF16),
            pltpu.VMEM((CAP, depth), BF16),
            pltpu.SemaphoreType.DMA((42,)),
        ],
        compiler_params=pltpu.CompilerParams(vmem_limit_bytes=60 * 1024 * 1024),
    )(routes[0], routes[1], x_here, rows_a, grad)


def solution(mesh):
    tokens = P("section", "ed", None)
    return jax.shard_map(
        functools.partial(shards, mesh.shape["section"]),
        mesh=mesh,
        in_specs=(tokens,) * 7
        + (P("section", None), P("section", None, "ed"), P("section", None, "ed"), P("section", "ed", None)),
        out_specs=(tokens, tokens),
        check_vma=False,
    )
```
